512 devices in a mesh: dp: 8 (over y, core), expert: 64 (over x, z).
Axes of the slice: x: 4, y: 4, z: 16, core: 2. Of those that a mesh axis runs over, the one named last changes fastest.
Arguments:
- activations: bfloat16 [1024, 8, 1536], P('expert', None, 'dp'), may hold values from -6 to 6
- w_down: bfloat16 [64, 1536, 4096], P('expert', 'dp'), may hold values from -0.15625 to 0.15625
- gate_weights: float32 [1024, 8], P('expert'), may hold values from 0.05 to 1
- cotangent: bfloat16 [1024, 4096], P('expert', 'dp'), may hold values from -0.59765625 to 0.59765625
- expert_ids: int32 [1024, 8], P('expert'), may hold values from 0 to 63, as said below
- replica_pick: int32 [1024, 8], P('expert'), may hold values from 0 to 1, as said below
- placement: int32 [16, 2], replicated, may hold values from 0 to 63, as said below
- group_cap: int32 [64], replicated, may hold values from 1 to 3, as said below
Outputs:
- combined: bfloat16 [1024, 4096], P('expert', 'dp')
- act_grad: bfloat16 [1024, 8, 1536], P('expert', None, 'dp')
- weight_grad: bfloat16 [64, 1536, 4096], P('expert', 'dp')
- gate_grad: float32 [1024, 8], P('expert')
The draws below stay inside these ranges and needn't reach their ends.
Inputs may be any that keep to these rules, and one draw needn't show every extreme that they name: `expert_ids`: each row names 8 different experts. One expert, drawn from the seed and without a replica, is named by every token; replicated experts are named more often than the others. `replica_pick`: read only for rows whose expert has a replica. `placement`: column 0 holds distinct experts, column 1 distinct indices of expert; no index hosts a replica of the expert it owns, and no expert owned by a host is itself replicated. `group_cap`: the expert named by every token has its owner's entry equal to 3.
All inputs are finite; a program needn't handle non-finite values.
Results may differ from the reference program's by a relative error of at most 0.02.
Values may be sent and summed in bfloat16 or wider, within the bound.
No kernel may reach another device: no remote copies, remote signals or barrier semaphores. Data moves between devices by JAX's collectives and lax.ppermute only.
A program may use at most 64 MiB of HBM per device.

```python
import math
import jax
import jax.numpy as jnp
from jax import lax

D = 4096
H = 1536
TOP = 8
TOK_BLK = 16
EXPERTS = 64
REPLICAS = 16
CAP = 3
TOKENS = 1024
N_DP = 8
N_EXPERT = 64


def move_into(order, value, target):
    position = jnp.argmax((order == value).astype(jnp.int32)).astype(jnp.int32)
    present = order[target]
    order = order.at[position].set(present)
    return order.at[target].set(value)


def routing_draws(key):
    base = jax.random.fold_in(key, 7)
    key_perm, key_score, key_pick, key_cap, key_slot = jax.random.split(base, 5)
    expert_order = jax.random.permutation(key_perm, EXPERTS).astype(jnp.int32)
    slot_pair = jax.random.randint(key_slot, (2,), 0, REPLICAS, dtype=jnp.int32)
    expert_order = move_into(expert_order, jnp.int32(0), 1 + slot_pair[0])
    expert_order = move_into(expert_order, jnp.int32(EXPERTS - 1), 1 + REPLICAS + slot_pair[1])
    always = expert_order[0]
    copied = expert_order[1:1 + REPLICAS]
    host_list = expert_order[1 + REPLICAS:1 + 2 * REPLICAS]
    tier_bias = jnp.zeros((EXPERTS,), jnp.int32).at[copied].set(1 << 19).at[always].set(3 << 20)
    noise = jax.random.randint(key_score, (TOKENS, EXPERTS), 0, 1 << 20, dtype=jnp.int32)
    score_table = (noise + tier_bias[None, :]) * EXPERTS + jnp.arange(EXPERTS, dtype=jnp.int32)[None, :]
    chosen = lax.top_k(score_table, TOP)[1].astype(jnp.int32)
    pick_bits = jax.random.randint(key_pick, (TOKENS, TOP), 0, 2, dtype=jnp.int32)
    cap_list = jax.random.randint(key_cap, (EXPERTS,), CAP // 2, CAP + 1, dtype=jnp.int32)
    cap_list = cap_list.at[always].set(CAP)
    placed = jnp.stack([copied, host_list], axis=1).astype(jnp.int32)
    return (chosen, pick_bits, placed, cap_list)


def draw_expert_ids(key, part):
    return routing_draws(key)[0]


def draw_replica_pick(key, part):
    return routing_draws(key)[1]


def draw_placement(key, part):
    return routing_draws(key)[2]


def draw_group_cap(key, part):
    return routing_draws(key)[3]


def block_levels(stream_key, shape, shards, smallest, largest):
    def one(dim, blocks):
        heights = jax.random.uniform(jax.random.fold_in(jax.random.fold_in(stream_key, 6), dim), (blocks,), jnp.float32, smallest / len(shards), largest / len(shards))
        return jnp.repeat(jnp.exp(heights), shape[dim] // blocks).reshape((-1,) + (1,) * (len(shape) - dim - 1))

    level = one(*shards[0])
    for cut in shards[1:]:
        level = level * one(*cut)
    return level


def bell_draw(stream_key, extent, scale, most, pieces=(), held_as=jnp.bfloat16):
    factor_of = block_levels(stream_key, extent, pieces, -0.22, 0.18) if pieces else 1.0
    array = jax.random.normal(stream_key, extent, jnp.float32) * scale * factor_of
    return jnp.minimum(jnp.maximum(array, -most), most).astype(held_as)


def setup_inputs(seed: int = 0) -> dict:
    streams_of = jax.random.split(jax.random.key(seed), 9)
    return {
        "activations": bell_draw(streams_of[0], (TOKENS, TOP, H), 1.0, 6.0, ((0, 64), (2, 8))),
        "w_down": bell_draw(streams_of[1], (EXPERTS, H, D), H ** -0.5, 0.15625, ((0, 64), (1, 8))),
        "gate_weights": jnp.clip(jnp.exp(math.log(1.0) - 2.9957323 * jax.random.uniform(streams_of[2], (TOKENS, TOP), jnp.float32) ** block_levels(streams_of[2], (TOKENS, TOP), ((0, 64),), -0.2, 0.2)), 0.05, 1.0),
        "cotangent": bell_draw(streams_of[3], (TOKENS, D), 0.1, 0.59765625, ((0, 64), (1, 8))),
        "expert_ids": draw_expert_ids(jax.random.fold_in(streams_of[8], 71), 0),
        "replica_pick": draw_replica_pick(jax.random.fold_in(streams_of[8], 71), 0),
        "placement": draw_placement(jax.random.fold_in(streams_of[8], 71), 0),
        "group_cap": draw_group_cap(jax.random.fold_in(streams_of[8], 71), 0),
    }


def routing_table(block_ids, block_pick, placement, group_cap):
    n_dev = group_cap.shape[0]
    flat_ids = block_ids.reshape(-1).astype(jnp.int32)
    flat_pick = block_pick.reshape(-1)
    match_copy = (flat_ids[:, None] == placement[None, :, 0]).astype(jnp.int32)
    has_copy = jnp.sum(match_copy, axis=1, dtype=jnp.int32)
    host_dev = jnp.sum(match_copy * placement[None, :, 1], axis=1, dtype=jnp.int32)
    to_copy = (has_copy > 0) & (flat_pick == 1)
    destination = jnp.where(to_copy, host_dev, flat_ids).astype(jnp.int32)
    row_kind = jnp.where(to_copy, 2, 1).astype(jnp.int32)
    onehot_dest = (destination[:, None] == jnp.arange(n_dev, dtype=jnp.int32)[None, :]).astype(jnp.int32)
    earlier = jnp.cumsum(onehot_dest, axis=0, dtype=jnp.int32) - onehot_dest
    row_rank = jnp.sum(earlier * onehot_dest, axis=1, dtype=jnp.int32)
    row_limit = jnp.sum(onehot_dest * group_cap[None, :], axis=1, dtype=jnp.int32)
    row_kept = row_rank < row_limit
    return destination, row_kind, row_rank, row_kept


def hosted(placement, n_dev):
    at_dev = (placement[:, 1][:, None] == jnp.arange(n_dev, dtype=jnp.int32)[None, :]).astype(jnp.int32)
    has_at = jnp.sum(at_dev, axis=0, dtype=jnp.int32)
    rep_at = jnp.sum(at_dev * placement[:, 0][:, None], axis=0, dtype=jnp.int32)
    return has_at, rep_at


def reference(activations, w_down, gate_weights, cotangent, expert_ids, replica_pick, placement, group_cap):
    blocks = N_EXPERT
    rows_blk = TOK_BLK * TOP
    ids_blk = expert_ids.reshape(blocks, TOK_BLK, TOP)
    pick_blk = replica_pick.reshape(blocks, TOK_BLK, TOP)
    destination, row_kind, row_rank, row_kept = jax.vmap(routing_table, in_axes=(0, 0, None, None))(ids_blk, pick_blk, placement, group_cap)
    slot_index = jnp.where(row_kept, destination * CAP + row_rank, blocks * CAP).astype(jnp.int32)
    source_all = jnp.broadcast_to(jnp.arange(blocks, dtype=jnp.int32)[:, None], (blocks, rows_blk))
    row_all = jnp.broadcast_to(jnp.arange(rows_blk, dtype=jnp.int32)[None, :], (blocks, rows_blk))
    inverse = jnp.full((blocks, blocks * CAP), -1, jnp.int32).at[source_all, slot_index].set(row_all, mode="drop")
    act_rows = activations.reshape(blocks, rows_blk, H)
    grad_rows = (gate_weights[:, :, None] * cotangent.astype(jnp.float32)[:, None, :]).astype(jnp.bfloat16).reshape(blocks, rows_blk, D)
    has_at, rep_at = hosted(placement, blocks)
    match_exp = (placement[:, 0][:, None] == jnp.arange(blocks, dtype=jnp.int32)[None, :]).astype(jnp.int32)
    has_of = jnp.sum(match_exp, axis=0, dtype=jnp.int32)
    host_of = jnp.sum(match_exp * placement[:, 1][:, None], axis=0, dtype=jnp.int32)
    source = jnp.arange(blocks, dtype=jnp.int32)[:, None]

    def gather_slots(dest_index):
        slot_rows = lax.dynamic_slice(inverse, (jnp.int32(0), (dest_index * CAP).astype(jnp.int32)), (blocks, CAP))
        valid_slot = slot_rows >= 0
        safe_pick = jnp.maximum(slot_rows, 0).astype(jnp.int32)
        inputs = jnp.where(valid_slot[:, :, None], act_rows[source, safe_pick], jnp.zeros((), act_rows.dtype)).reshape(blocks * CAP, H)
        slot_kinds = jnp.where(valid_slot, row_kind[source, safe_pick], 0).reshape(blocks * CAP)
        slot_grads = jnp.where(valid_slot[:, :, None], grad_rows[source, safe_pick], jnp.zeros((), grad_rows.dtype)).reshape(blocks * CAP, D)
        return inputs, slot_kinds, slot_grads

    def sliced(inputs, weight):
        left = inputs.astype(jnp.float32).reshape(-1, N_DP, H // N_DP)
        right = weight.astype(jnp.float32).reshape(N_DP, H // N_DP, D)
        return jnp.einsum("sih,ihd->sid", left, right)

    def forward_dest(dest_index):
        inputs, slot_kinds, slot_grads = gather_slots(dest_index)
        own_in = jnp.where((slot_kinds == 1)[:, None], inputs, jnp.zeros((), inputs.dtype))
        copy_in = jnp.where((slot_kinds == 2)[:, None], inputs, jnp.zeros((), inputs.dtype))
        w_own = w_down[dest_index]
        w_copy = w_down[rep_at[dest_index]]
        part = (sliced(own_in, w_own) + sliced(copy_in, w_copy)).astype(jnp.bfloat16)
        total = jnp.sum(part.astype(jnp.float32), axis=1)
        back_own = jnp.einsum("sd,hd->sh", slot_grads.astype(jnp.float32), w_own.astype(jnp.float32))
        back_copy = jnp.einsum("sd,hd->sh", slot_grads.astype(jnp.float32), w_copy.astype(jnp.float32))
        input_back = jnp.where((slot_kinds == 1)[:, None], back_own, jnp.where((slot_kinds == 2)[:, None], back_copy, jnp.float32(0.0))).astype(jnp.bfloat16)
        return total.reshape(blocks, CAP, D), input_back.reshape(blocks, CAP, H)

    totals, input_backs = lax.map(forward_dest, jnp.arange(blocks, dtype=jnp.int32))

    def weight_for(expert_index):
        inputs, slot_kinds, slot_grads = gather_slots(expert_index)
        own_in = jnp.where((slot_kinds == 1)[:, None], inputs, jnp.zeros((), inputs.dtype))
        own_grad = jnp.einsum("sh,sd->hd", own_in.astype(jnp.float32), slot_grads.astype(jnp.float32))
        host_inputs, host_kinds, host_grads = gather_slots(host_of[expert_index])
        copy_in = jnp.where((host_kinds == 2)[:, None], host_inputs, jnp.zeros((), host_inputs.dtype))
        copy_grad = jnp.einsum("sh,sd->hd", copy_in.astype(jnp.float32), host_grads.astype(jnp.float32)).astype(jnp.bfloat16)
        copy_grad = jnp.where(has_of[expert_index] > 0, copy_grad, jnp.zeros((), copy_grad.dtype))
        return (own_grad + copy_grad.astype(jnp.float32)).astype(jnp.bfloat16)

    weight_grad = lax.map(weight_for, jnp.arange(blocks, dtype=jnp.int32))
    safe_rank = jnp.minimum(row_rank, CAP - 1).astype(jnp.int32)
    row_out = jnp.where(row_kept[:, :, None], totals[destination, source_all, safe_rank], jnp.float32(0.0)).reshape(TOKENS, TOP, D)
    combined = jnp.sum(gate_weights[:, :, None] * row_out, axis=1).astype(jnp.bfloat16)
    gate_grad = jnp.sum(cotangent.astype(jnp.float32)[:, None, :] * row_out, axis=2)
    act_grad = jnp.where(row_kept[:, :, None], input_backs[destination, source_all, safe_rank], jnp.zeros((), input_backs.dtype)).reshape(TOKENS, TOP, H)
    return combined, act_grad, weight_grad, gate_grad
```

```python
import jax
import jax.numpy as jnp
from jax import lax
from jax.experimental import pallas as pl
from jax.experimental.pallas import tpu as pltpu
from jax.sharding import PartitionSpec as P

CAP = 3
SLOTS = 2 * CAP
NY = 4
BF = jnp.bfloat16
F32 = jnp.float32
VM = pl.BlockSpec(memory_space=pltpu.VMEM)
SM = pl.BlockSpec(memory_space=pltpu.SMEM)


def call(kernel, outs, specs, flops=0, moved=1 << 20):
    return pl.pallas_call(
        kernel,
        out_shape=outs,
        in_specs=specs,
        out_specs=jax.tree.map(lambda _: VM, outs),
        compiler_params=pltpu.CompilerParams(vmem_limit_bytes=40 << 20),
        cost_estimate=pl.CostEstimate(flops=flops, bytes_accessed=moved, transcendentals=0),
    )


def dot(a, b, ca, cb):
    return lax.dot_general(a, b, (((ca,), (cb,)), ((), ())), preferred_element_type=F32)


def shape(dims, dtype=BF):
    return jax.ShapeDtypeStruct(dims, dtype)


def send(value, step, other):
    pairs = [(i, ((i // 2 + step) % NY) * 2 + ((i % 2) ^ other)) for i in range(2 * NY)]
    return lax.ppermute(value, "dp", pairs)


def peer_column(here, step, other, width):
    peer = lax.rem(here // 2 + step, NY) * 2 + (lax.rem(here, 2) + other) % 2
    return pl.multiple_of(peer * width, width)


def cut_weights(here_ref, w_ref, *outs):
    width = outs[0].shape[1]
    here = here_ref[0]
    for step in range(NY):
        for other in range(2):
            at = peer_column(here, step, other, width)
            outs[2 * step + other][...] = w_ref[:, pl.ds(at, width)]


def join_gradient(here_ref, *refs):
    parts, out_ref = refs[:-1], refs[-1]
    width = parts[0].shape[1]
    here = here_ref[0]
    for step in range(NY):
        for other in range(2):
            at = peer_column(here, (NY - step) % NY, other, width)
            out_ref[:, pl.ds(at, width)] = parts[2 * step + other][...]


def dispatch(
    id_row_ref, id_col_ref, pick_row_ref, pick_col_ref, place_ref, place_t_ref, cap_ref,
    act_ref, cot_ref, gate_ref, sent_ref, slot_ref,
):
    n_dev = cap_ref.shape[0]
    rows, hidden = act_ref.shape
    toks, feats = cot_ref.shape
    top = rows // toks
    id_row, id_col = id_row_ref[...], id_col_ref[...]
    match = (place_ref[:, 0:1] == id_row).astype(jnp.int32)
    has = jnp.sum(match, axis=0, keepdims=True)
    host = jnp.sum(match * place_ref[:, 1:2], axis=0, keepdims=True)
    copy_row = (has > 0) & (pick_row_ref[...] == 1)
    dest_row = jnp.where(copy_row, host, id_row)
    match_t = (place_t_ref[0:1, :] == id_col).astype(jnp.int32)
    has_t = jnp.sum(match_t, axis=1, keepdims=True)
    host_t = jnp.sum(match_t * place_t_ref[1:2, :], axis=1, keepdims=True)
    dest_col = jnp.where((has_t > 0) & (pick_col_ref[...] == 1), host_t, id_col)
    before = lax.broadcasted_iota(jnp.int32, (rows, rows), 0) < lax.broadcasted_iota(
        jnp.int32, (rows, rows), 1
    )
    same = (dest_col == dest_row) & before
    rank = jnp.sum(same.astype(jnp.int32), axis=0, keepdims=True)
    at_dest = lax.broadcasted_iota(jnp.int32, (n_dev, rows), 0) == dest_row
    limit = jnp.sum(jnp.where(at_dest, cap_ref[...], 0), axis=0, keepdims=True)
    place = (jnp.where(copy_row, CAP, 0) + rank) * n_dev + id_row
    slot = jnp.where(rank < limit, place, -1)
    slot_ref[...] = slot
    pick = lax.broadcasted_iota(jnp.int32, (SLOTS * n_dev, rows), 0) == slot
    pick = pick.astype(F32).astype(BF)
    act_s = dot(pick, act_ref[...], 1, 0)
    owner = lax.broadcasted_iota(jnp.int32, (rows, toks), 0) // top == lax.broadcasted_iota(
        jnp.int32, (rows, toks), 1
    )
    cot = dot(owner.astype(F32).astype(BF), cot_ref[...], 1, 0)
    grad = (gate_ref[...] * cot).astype(BF)
    grad_s = dot(pick, grad, 1, 0)
    base = SLOTS * feats
    for j in range(SLOTS):
        part = slice(j * n_dev, (j + 1) * n_dev)
        sent_ref[:, j * feats : (j + 1) * feats] = grad_s[part].astype(BF)
        sent_ref[:, base + j * hidden : base + (j + 1) * hidden] = act_s[part].astype(BF)


def backward(got_ref, *refs):
    w_refs = refs[: 2 * NY]
    act_ref, grad_ref, mine_ref, theirs_ref = refs[2 * NY :]
    n_dev = got_ref.shape[0]
    feats, hidden = grad_ref.shape[1], act_ref.shape[0]
    base = SLOTS * feats
    acts = []
    for j in range(SLOTS):
        part = slice(j * n_dev, (j + 1) * n_dev)
        grad_ref[part, :] = got_ref[:, j * feats : (j + 1) * feats]
        acts.append(got_ref[:, base + j * hidden : base + (j + 1) * hidden].astype(F32))
    act_ref[...] = jnp.concatenate(acts, axis=0).T.astype(BF)
    grad = grad_ref[...]
    for step in range(NY):
        mine_ref[step] = dot(w_refs[2 * step][...], grad, 1, 1).astype(BF)
        theirs_ref[step] = dot(w_refs[2 * step + 1][...], grad, 1, 1).astype(BF)


def add_cores(mine_ref, theirs_ref, *outs):
    for step in range(NY):
        outs[step][...] = (mine_ref[step].astype(F32) + theirs_ref[step].astype(F32)).astype(BF)


def forward(near_ref, far_ref, *refs):
    w_refs = refs[: 2 * NY]
    backs = refs[2 * NY : 3 * NY]
    sent_ref = refs[-1]
    n_dev = sent_ref.shape[0]
    feats = w_refs[0].shape[1]
    hidden = near_ref.shape[1]
    total = None
    for step in range(NY):
        for other, acts in enumerate((near_ref, far_ref)):
            part = dot(acts[step], w_refs[2 * step + other][...], 0, 0)
            total = part if total is None else total + part
    back = backs[0][...].astype(F32)
    for step in range(1, NY):
        back = back + backs[step][...].astype(F32)
    back = back.T.astype(BF)
    base = SLOTS * feats
    for j in range(SLOTS):
        part = slice(j * n_dev, (j + 1) * n_dev)
        sent_ref[:, j * feats : (j + 1) * feats] = total[part].astype(BF)
        sent_ref[:, base + j * hidden : base + (j + 1) * hidden] = back[part]


def weights_back(near_ref, far_ref, grad_ref, *outs):
    grad = grad_ref[...]
    for step in range(NY):
        outs[2 * step][...] = dot(near_ref[step], grad, 1, 0).astype(BF)
        outs[2 * step + 1][...] = dot(far_ref[step], grad, 1, 0).astype(BF)


def collect(got_ref, slot_ref, act_ref, gate_ref, mixed_ref, back_ref, gate_out_ref):
    n_dev = got_ref.shape[0]
    rows, hidden = act_ref.shape
    toks, feats = mixed_ref.shape
    base = SLOTS * feats
    pick = lax.broadcasted_iota(jnp.int32, (rows, SLOTS * n_dev), 1) == slot_ref[...]
    pick = pick.astype(F32).astype(BF)
    outs = jnp.concatenate(
        [got_ref[:, j * feats : (j + 1) * feats] for j in range(SLOTS)], axis=0
    )
    backs = jnp.concatenate(
        [got_ref[:, base + j * hidden : base + (j + 1) * hidden] for j in range(SLOTS)], axis=0
    )
    gate = gate_ref[...]
    row_out = dot(pick, outs, 1, 0) * gate
    mixed_ref[...] = jnp.sum(row_out.reshape(toks, rows // toks, feats), axis=1).astype(BF)
    back = dot(pick, backs, 1, 0)
    back_ref[...] = back.astype(BF)
    gate_out_ref[...] = jnp.sum(back * act_ref[...].astype(F32), axis=1, keepdims=True) / gate


def on_device(acts, w_down, gates, cotangent, expert_ids, replica_pick, placement, group_cap):
    n_dev = lax.axis_size("expert")
    toks, top, hidden = acts.shape
    feats = cotangent.shape[1]
    rows, slots = toks * top, SLOTS * n_dev
    here = lax.axis_index("dp").astype(jnp.int32).reshape(1)
    flat_act = acts.reshape(rows, hidden)
    gate_col = gates.reshape(rows, 1)
    ids, picks = expert_ids.astype(jnp.int32), replica_pick.astype(jnp.int32)

    cuts = call(cut_weights, [shape((hidden, feats))] * (2 * NY), [SM, VM], moved=3 << 20)(
        here, w_down[0]
    )
    weights = [None] * (2 * NY)
    for step in range(NY):
        for other in range(2):
            piece = cuts[2 * step + other]
            if step or other:
                piece = send(piece, step, other)
            weights[2 * ((NY - step) % NY) + other] = piece

    width = SLOTS * (feats + hidden)
    sent, slot_row = call(
        dispatch, [shape((n_dev, width)), shape((1, rows), jnp.int32)], [VM] * 10
    )(
        ids.reshape(1, rows), ids.reshape(rows, 1), picks.reshape(1, rows), picks.reshape(rows, 1),
        placement, placement.T, group_cap.reshape(n_dev, 1), flat_act, cotangent, gate_col,
    )
    got = lax.all_to_all(sent, "expert", 0, 0, tiled=True)

    block = shape((hidden, slots))
    flops = 2 * slots * feats * hidden * 2 * NY
    own_act, grad, mine, theirs = call(
        backward,
        [block, shape((slots, feats)), shape((NY, hidden, slots)), shape((NY, hidden, slots))],
        [VM] * (1 + 2 * NY),
        flops=flops,
    )(got, *weights)
    theirs = send(theirs, 0, 1)
    near = jnp.stack([own_act] + [send(own_act, NY - step, 0) for step in range(1, NY)])
    sums = call(add_cores, [block] * NY, [VM, VM])(mine, theirs)
    far = send(near, 0, 1)
    backs = [sums[0]] + [send(sums[step], step, 0) for step in range(1, NY)]
    returned = call(forward, shape((n_dev, width)), [VM] * (2 + 3 * NY), flops=flops)(
        near, far, *weights, *backs
    )
    home = lax.all_to_all(returned, "expert", 0, 0, tiled=True)

    pieces = call(weights_back, [shape((hidden, feats))] * (2 * NY), [VM] * 3, flops=flops)(
        near, far, grad
    )
    joined = []
    for step in range(NY):
        for other in range(2):
            piece = pieces[2 * step + other]
            joined.append(send(piece, step, other) if step or other else piece)
    weight_grad = call(
        join_gradient, shape((hidden, 2 * NY * feats)), [SM] + [VM] * (2 * NY), moved=3 << 20
    )(here, *joined)

    combined, back_rows, gate_part = call(
        collect,
        [shape((toks, feats)), shape((rows, hidden)), shape((rows, 1), F32)],
        [VM] * 4,
    )(home, slot_row.reshape(rows, 1), flat_act, gate_col)
    gate_grad = lax.psum(gate_part.reshape(toks, top), "dp")
    return combined, back_rows.reshape(toks, top, hidden), weight_grad[None], gate_grad


def solution(mesh):
    return jax.shard_map(
        on_device,
        mesh=mesh,
        in_specs=(
            P("expert", None, "dp"),
            P("expert", "dp", None),
            P("expert", None),
            P("expert", "dp"),
            P("expert", None),
            P("expert", None),
            P(),
            P(),
        ),
        out_specs=(
            P("expert", "dp"),
            P("expert", None, "dp"),
            P("expert", "dp", None),
            P("expert", None),
        ),
        check_vma=False,
    )
```

```python
import jax
import jax.numpy as jnp
from jax import lax
from jax.experimental import pallas as pl
from jax.experimental.pallas import tpu as pltpu
from jax.sharding import PartitionSpec as P

CAP = 3
SLOTS = 2 * CAP
ROWS = 8
NY = 4
EXTRA = 16
BF = jnp.bfloat16
F32 = jnp.float32
VM = pl.BlockSpec(memory_space=pltpu.VMEM)
SM = pl.BlockSpec(memory_space=pltpu.SMEM)


def call(kernel, outs, specs, flops=0, moved=1 << 20, scratch=()):
    return pl.pallas_call(
        kernel,
        out_shape=outs,
        in_specs=specs,
        out_specs=jax.tree.map(lambda _: VM, outs),
        scratch_shapes=list(scratch),
        compiler_params=pltpu.CompilerParams(vmem_limit_bytes=40 << 20),
        cost_estimate=pl.CostEstimate(flops=flops, bytes_accessed=moved, transcendentals=0),
    )


def dot(a, b, ca, cb):
    return lax.dot_general(a, b, (((ca,), (cb,)), ((), ())), preferred_element_type=F32)


def shape(dims, dtype=BF):
    return jax.ShapeDtypeStruct(dims, dtype)


def ones(mask):
    return mask.astype(F32).astype(BF)


def iota(dims, axis):
    return lax.broadcasted_iota(jnp.int32, dims, axis)


def payload_width(feats, hidden):
    return (max(feats + EXTRA, CAP * hidden) + 127) // 128 * 128


def send(value, step, other):
    pairs = [(i, ((i // 2 + step) % NY) * 2 + ((i % 2) ^ other)) for i in range(2 * NY)]
    return lax.ppermute(value, "dp", pairs)


def exchange_y(value):
    groups = [[2 * y + core for y in range(NY)] for core in range(2)]
    return lax.all_to_all(value, "dp", 0, 0, axis_index_groups=groups, tiled=True)


def chip(here, step):
    return lax.rem(here // 2 + step, NY)


def peer_column(here, step, other, width):
    peer = chip(here, step) * 2 + lax.rem(lax.rem(here, 2) + other, 2)
    return pl.multiple_of(peer * width, width)


def cut_weights(here_ref, w_ref, *outs):
    width = outs[0].shape[1]
    here = here_ref[0]
    for step in range(NY):
        for other in range(2):
            at = peer_column(here, step, other, width)
            outs[2 * step + other][...] = w_ref[:, pl.ds(at, width)]


def join_gradient(here_ref, *refs):
    parts, out_ref = refs[:-1], refs[-1]
    width = parts[0].shape[1]
    here = here_ref[0]
    for step in range(NY):
        for other in range(2):
            at = peer_column(here, (NY - step) % NY, other, width)
            out_ref[:, pl.ds(at, width)] = parts[2 * step + other][...]


def column(stored):
    top, toks = stored.shape
    spread = jnp.broadcast_to(stored[None], (toks, top, toks)).reshape(toks * top, toks)
    mine = iota(spread.shape, 0) // top == iota(spread.shape, 1)
    return jnp.sum(jnp.where(mine, spread, jnp.zeros_like(spread)), axis=1, keepdims=True)


def as_row(col):
    n = col.shape[0]
    diagonal = iota((n, n), 0) == iota((n, n), 1)
    return jnp.sum(jnp.where(diagonal, col, jnp.zeros_like(col)), axis=0, keepdims=True)


def split_slot(slot):
    expert, j = slot >> 3, slot & 7
    kind = (j >= CAP).astype(jnp.int32)
    return j - CAP * kind, expert * ROWS + SLOTS + kind


def dispatch(
    ids_ref, picks_ref, place_ref, cap_ref, act_ref, cot_ref, gate_ref, sent_ref, slot_ref, right_ref
):
    n_dev = cap_ref.shape[1]
    rows, hidden = act_ref.shape
    toks, feats = cot_ref.shape
    top = rows // toks
    ids, picks = column(ids_ref[...]), column(picks_ref[...])
    match = (place_ref[0:1, :] == ids).astype(jnp.int32)
    has = jnp.sum(match, axis=1, keepdims=True)
    host = jnp.sum(match * place_ref[1:2, :], axis=1, keepdims=True)
    copied = (has > 0) & (picks == 1)
    dest = jnp.where(copied, host, ids)
    dest_row = as_row(dest)
    earlier = (dest == dest_row) & (iota((rows, rows), 1) < iota((rows, rows), 0))
    rank = jnp.sum(earlier.astype(jnp.int32), axis=1, keepdims=True)
    at_dest = iota((rows, n_dev), 1) == dest
    limit = jnp.sum(jnp.where(at_dest, cap_ref[...], 0), axis=1, keepdims=True)
    slot = jnp.where(rank < limit, ids * ROWS + jnp.where(copied, CAP, 0) + rank, -1)
    slot_ref[...] = slot

    slot_row = as_row(slot)
    rank_row, act_row = split_slot(slot_row)
    q = iota((ROWS * n_dev, rows), 0)
    left = [q == slot_row] + [(q == act_row) & (rank_row == r) for r in range(CAP)]
    owner = ones(iota((rows, toks), 0) // top == iota((rows, toks), 1))
    grad = column(gate_ref[...]) * dot(owner, cot_ref[...], 1, 0)
    right_ref[...] = jnp.zeros_like(right_ref)
    right_ref[:rows, :feats] = grad.astype(BF)
    for r in range(CAP):
        right_ref[(1 + r) * rows : (2 + r) * rows, r * hidden : (r + 1) * hidden] = act_ref[...]
    total = None
    for i, mask in enumerate(left):
        part = dot(ones(mask), right_ref[i * rows : (i + 1) * rows, :], 1, 0)
        total = part if total is None else total + part
    sent_ref[...] = total.astype(BF)


def slot_masks(n_dev, q_axis):
    dims = [SLOTS * n_dev, SLOTS * n_dev]
    dims[q_axis] = ROWS * n_dev
    q, s = iota(dims, q_axis), iota(dims, 1 - q_axis)
    j, source = s // n_dev, lax.rem(s, n_dev)
    kind = (j >= CAP).astype(jnp.int32)
    wide = q == source * ROWS + j
    narrow = q == source * ROWS + SLOTS + kind
    return wide, [narrow & (j - CAP * kind == r) for r in range(CAP)]


def unpack(got_ref, act_ref, grad_ref):
    n_dev = got_ref.shape[0] // ROWS
    feats, hidden = grad_ref.shape[1], act_ref.shape[1]
    wide, _ = slot_masks(n_dev, 1)
    _, narrow = slot_masks(n_dev, 0)
    total = None
    for r in range(CAP):
        part = dot(got_ref[:, r * hidden : (r + 1) * hidden], ones(narrow[r]), 0, 0)
        total = part if total is None else total + part
    for y in range(NY):
        act_ref[y] = total.astype(BF)
    grad_ref[...] = dot(ones(wide), got_ref[:, :feats], 1, 0).astype(BF)


def backward(here_ref, grad_ref, *refs):
    w_refs, (mine_ref, theirs_ref) = refs[:-2], refs[-2:]
    grad = grad_ref[...]
    for step in range(NY):
        at = chip(here_ref[0], step)
        mine_ref[at] = dot(w_refs[2 * step][...], grad, 1, 1).astype(BF)
        theirs_ref[at] = dot(w_refs[2 * step + 1][...], grad, 1, 1).astype(BF)


def add_cores(near_ref, mine_ref, theirs_ref, out_ref):
    hidden, slots = near_ref.shape[1:]
    gate = jnp.zeros((1, slots), F32)
    for y in range(NY):
        both = mine_ref[y].astype(F32) + theirs_ref[y].astype(F32)
        gate = gate + jnp.sum(near_ref[y].astype(F32) * both, axis=0, keepdims=True)
        out_ref[y, :hidden] = both.astype(BF)
    extra = two_parts(gate)
    for y in range(NY):
        out_ref[y, hidden:] = extra


def two_parts(row):
    high = row.astype(BF).astype(F32)
    at = iota((EXTRA, row.shape[1]), 0)
    return jnp.where(at == 0, high, jnp.where(at == 1, row - high, 0.0)).astype(BF)


def forward(here_ref, near_ref, far_ref, back_ref, *refs):
    w_refs, (sent_ref, sum_ref) = refs[:-2], refs[-2:]
    n_dev = sent_ref.shape[0] // ROWS
    feats, hidden = w_refs[0].shape[1], near_ref.shape[1]
    total = None
    for step in range(NY):
        at = chip(here_ref[0], step)
        for other, acts in enumerate((near_ref, far_ref)):
            part = dot(acts[at], w_refs[2 * step + other][...], 0, 0)
            total = part if total is None else total + part
    back = sum(back_ref[y].astype(F32) for y in range(NY))
    gate = jnp.sum(back[hidden:], axis=0, keepdims=True)
    back = back[:hidden].astype(BF)
    wide, narrow = slot_masks(n_dev, 0)
    wide = ones(wide)
    sum_ref[...] = jnp.zeros_like(sum_ref)
    sum_ref[:, :feats] = dot(wide, total.astype(BF), 1, 0)
    sum_ref[:, feats : feats + EXTRA] = dot(wide, two_parts(gate), 1, 1)
    for r in range(CAP):
        sum_ref[:, r * hidden : (r + 1) * hidden] += dot(ones(narrow[r]), back, 1, 1)
    sent_ref[...] = sum_ref[...].astype(BF)


def weights_back(here_ref, near_ref, far_ref, grad_ref, *outs):
    grad = grad_ref[...]
    for step in range(NY):
        at = chip(here_ref[0], step)
        outs[2 * step][...] = dot(near_ref[at], grad, 1, 0).astype(BF)
        outs[2 * step + 1][...] = dot(far_ref[at], grad, 1, 0).astype(BF)


def collect(got_ref, slot_ref, gate_ref, mixed_ref, back_ref, gate_out_ref):
    top, toks = gate_ref.shape
    rows, hidden = back_ref.shape
    feats = mixed_ref.shape[1]
    gate = column(gate_ref[...])
    slot = slot_ref[...]
    rank, act_row = split_slot(slot)
    q = iota((rows, got_ref.shape[0]), 1)
    wide = ones(q == slot)
    row_out = dot(wide, got_ref[:, :feats], 1, 0) * gate
    mixed_ref[...] = jnp.sum(row_out.reshape(toks, top, feats), axis=1).astype(BF)
    back = None
    for r in range(CAP):
        pick = ones((q == act_row) & (rank == r))
        part = dot(pick, got_ref[:, r * hidden : (r + 1) * hidden], 1, 0)
        back = part if back is None else back + part
    back_ref[...] = back.astype(BF)
    extra = dot(wide, got_ref[:, feats:], 1, 0)
    gate_back = jnp.sum(jnp.where(iota(extra.shape, 1) < 2, extra, 0.0), axis=1, keepdims=True) / gate
    at_tok = iota((rows, toks), 0) // top == iota((rows, toks), 1)
    spread = jnp.where(at_tok, gate_back, 0.0)
    gate_out_ref[...] = jnp.sum(spread.reshape(toks, top, toks), axis=0)


def on_device(acts, w_down, gates, cotangent, expert_ids, replica_pick, placement, group_cap):
    n_dev = lax.axis_size("expert")
    toks, top, hidden = acts.shape
    feats = cotangent.shape[1]
    rows, slots = toks * top, SLOTS * n_dev
    width = payload_width(feats, hidden)
    here = lax.axis_index("dp").astype(jnp.int32).reshape(1)
    gates_t = gates.T
    pieces_shape = [shape((hidden, feats))] * (2 * NY)

    cuts = call(cut_weights, pieces_shape, [SM, VM], moved=3 << 20)(here, w_down[0])
    weights = [None] * (2 * NY)
    for step in range(NY):
        for other in range(2):
            piece = cuts[2 * step + other]
            if step or other:
                piece = send(piece, step, other)
            weights[2 * ((NY - step) % NY) + other] = piece

    sent, slot = call(
        dispatch,
        [shape((ROWS * n_dev, width)), shape((rows, 1), jnp.int32)],
        [VM] * 7,
        scratch=[pltpu.VMEM(((1 + CAP) * rows, width), BF)],
    )(
        expert_ids.T, replica_pick.T, placement.T, group_cap.reshape(1, n_dev),
        acts.reshape(rows, hidden), cotangent, gates_t,
    )

    def exchange(value):
        value = value.reshape(n_dev, ROWS, width)
        return lax.all_to_all(value, "expert", 0, 0, tiled=True).reshape(ROWS * n_dev, width)

    got = exchange(sent)
    stack = shape((NY, hidden, slots))
    flops = 2 * slots * feats * hidden * 2 * NY
    near, grad = call(unpack, [stack, shape((slots, feats))], [VM])(got)
    near = exchange_y(near)
    mine, theirs = call(backward, [stack] * 2, [SM] + [VM] * (1 + 2 * NY), flops=flops)(
        here, grad, *weights
    )
    theirs = send(theirs, 0, 1)
    back = call(add_cores, shape((NY, hidden + EXTRA, slots)), [VM] * 3)(near, mine, theirs)
    far = send(near, 0, 1)
    back = exchange_y(back)
    returned = call(
        forward,
        shape((ROWS * n_dev, width)),
        [SM] + [VM] * (3 + 2 * NY),
        flops=flops,
        scratch=[pltpu.VMEM((ROWS * n_dev, width), F32)],
    )(here, near, far, back, *weights)
    home = exchange(returned)

    pieces = call(weights_back, pieces_shape, [SM] + [VM] * 3, flops=flops)(here, near, far, grad)
    joined = []
    for step in range(NY):
        for other in range(2):
            piece = pieces[2 * step + other]
            joined.append(send(piece, step, other) if step or other else piece)
    weight_grad = call(
        join_gradient, shape((hidden, 2 * NY * feats)), [SM] + [VM] * (2 * NY), moved=3 << 20
    )(here, *joined)

    combined, back_rows, gate_part = call(
        collect,
        [shape((toks, feats)), shape((rows, hidden)), shape((top, toks), F32)],
        [VM] * 3,
    )(home, slot, gates_t)
    gate_grad = (gate_part + send(gate_part, 0, 1)).T
    return combined, back_rows.reshape(toks, top, hidden), weight_grad[None], gate_grad


def solution(mesh):
    return jax.shard_map(
        on_device,
        mesh=mesh,
        in_specs=(
            P("expert", None, "dp"),
            P("expert", "dp", None),
            P("expert", None),
            P("expert", "dp"),
            P("expert", None),
            P("expert", None),
            P(),
            P(),
        ),
        out_specs=(
            P("expert", "dp"),
            P("expert", None, "dp"),
            P("expert", "dp", None),
            P("expert", None),
        ),
        check_vma=False,
    )
```

```python
import jax
import jax.numpy as jnp
from jax import lax
from jax.experimental import pallas as pl
from jax.experimental.pallas import tpu as pltpu
from jax.sharding import PartitionSpec as P

CAP = 3
SLOTS = 2 * CAP
LANES = 128
TILE = 4
NY = 4
BF = jnp.bfloat16
F32 = jnp.float32
VM = pl.BlockSpec(memory_space=pltpu.VMEM)
SM = pl.BlockSpec(memory_space=pltpu.SMEM)


def call(kernel, outs, specs, flops=0, moved=1 << 20, scratch=(), vmem=40 << 20):
    return pl.pallas_call(
        kernel,
        out_shape=outs,
        in_specs=specs,
        out_specs=jax.tree.map(lambda _: VM, outs),
        scratch_shapes=list(scratch),
        compiler_params=pltpu.CompilerParams(vmem_limit_bytes=vmem),
        cost_estimate=pl.CostEstimate(flops=flops, bytes_accessed=moved, transcendentals=0),
    )


def dot(a, b, ca, cb):
    return lax.dot_general(a, b, (((ca,), (cb,)), ((), ())), preferred_element_type=F32)


def shape(dims, dtype=BF):
    return jax.ShapeDtypeStruct(dims, dtype)


def ones(mask):
    return mask.astype(F32).astype(BF)


def iota(dims, axis):
    return lax.broadcasted_iota(jnp.int32, dims, axis)


def payload_rows(feats, hidden):
    wide = SLOTS * feats // LANES
    narrow = -(-SLOTS * hidden // LANES)
    return wide, narrow, -(-(wide + narrow) // TILE) * TILE


def send(value, step, other):
    pairs = [(i, ((i // 2 + step) % NY) * 2 + ((i % 2) ^ other)) for i in range(2 * NY)]
    return lax.ppermute(value, "dp", pairs)


def exchange_y(value):
    groups = [[2 * y + core for y in range(NY)] for core in range(2)]
    return lax.all_to_all(value, "dp", 0, 0, axis_index_groups=groups, tiled=True)


def chip(here, step):
    return lax.rem(here // 2 + step, NY)


def peer_column(here, step, other, width):
    peer = chip(here, step) * 2 + lax.rem(lax.rem(here, 2) + other, 2)
    return pl.multiple_of(peer * width, width)


def cut_weights(here_ref, w_ref, *outs):
    width = outs[0].shape[1]
    here = here_ref[0]
    for step in range(NY):
        for other in range(2):
            at = peer_column(here, step, other, width)
            outs[2 * step + other][...] = w_ref[:, pl.ds(at, width)]


def join_gradient(here_ref, *refs):
    parts, out_ref = refs[:-1], refs[-1]
    width = parts[0].shape[1]
    here = here_ref[0]
    for step in range(NY):
        for other in range(2):
            at = peer_column(here, (NY - step) % NY, other, width)
            out_ref[:, pl.ds(at, width)] = parts[2 * step + other][...]


def column(stored):
    top, toks = stored.shape
    spread = jnp.broadcast_to(stored[None], (toks, top, toks)).reshape(toks * top, toks)
    mine = iota(spread.shape, 0) // top == iota(spread.shape, 1)
    return jnp.sum(jnp.where(mine, spread, jnp.zeros_like(spread)), axis=1, keepdims=True)


def as_row(col):
    n = col.shape[0]
    diagonal = iota((n, n), 0) == iota((n, n), 1)
    return jnp.sum(jnp.where(diagonal, col, jnp.zeros_like(col)), axis=0, keepdims=True)


def pack(rows_ref, flat_ref, wide_vals, narrow_vals):
    n_dev = flat_ref.shape[0]
    feats, hidden = wide_vals.shape[1], narrow_vals.shape[1]
    wide, narrow, rows = payload_rows(feats, hidden)
    each = feats // LANES
    for j in range(SLOTS):
        part = slice(j * n_dev, (j + 1) * n_dev)
        for i in range(each):
            block = wide_vals[part, i * LANES : (i + 1) * LANES]
            rows_ref[pl.ds(j * each + i, n_dev, stride=rows), :] = block
        flat_ref[:, j * hidden : (j + 1) * hidden] = narrow_vals[part]
    for i in range(rows - wide):
        block = jnp.zeros((n_dev, LANES), F32)
        if i < narrow:
            block = flat_ref[:, i * LANES : (i + 1) * LANES]
        rows_ref[pl.ds(wide + i, n_dev, stride=rows), :] = block


def unpack(rows_ref, flat_ref, feats, hidden):
    n_dev = flat_ref.shape[0]
    wide, narrow, rows = payload_rows(feats, hidden)
    each = feats // LANES
    wide_vals = jnp.concatenate(
        [
            jnp.concatenate(
                [rows_ref[pl.ds(j * each + i, n_dev, stride=rows), :] for i in range(each)], axis=1
            )
            for j in range(SLOTS)
        ],
        axis=0,
    )
    for i in range(narrow):
        block = rows_ref[pl.ds(wide + i, n_dev, stride=rows), :]
        flat_ref[:, i * LANES : (i + 1) * LANES] = block
    narrow_vals = jnp.concatenate(
        [flat_ref[:, j * hidden : (j + 1) * hidden] for j in range(SLOTS)], axis=0
    )
    return wide_vals, narrow_vals


def dispatch(
    ids_hbm, picks_hbm, place_hbm, cap_hbm, act_hbm, cot_hbm, gate_hbm, sent_ref, slot_ref,
    ids_ref, picks_ref, place_ref, cap_ref, act_ref, cot_ref, gate_ref, rows_ref, flat_ref, sems,
):
    sources = (ids_hbm, picks_hbm, place_hbm, cap_hbm, act_hbm, cot_hbm, gate_hbm)
    targets = (ids_ref, picks_ref, place_ref, cap_ref, act_ref, cot_ref, gate_ref)
    copies = [
        pltpu.make_async_copy(source, target, sems.at[i])
        for i, (source, target) in enumerate(zip(sources, targets))
    ]
    for copy in copies:
        copy.start()
    for copy in copies:
        copy.wait()
    n_dev = cap_ref.shape[1]
    rows, hidden = act_ref.shape
    toks, feats = cot_ref.shape
    top = rows // toks
    ids, picks = column(ids_ref[...]), column(picks_ref[...])
    match = (place_ref[0:1, :] == ids).astype(jnp.int32)
    has = jnp.sum(match, axis=1, keepdims=True)
    host = jnp.sum(match * place_ref[1:2, :], axis=1, keepdims=True)
    copied = (has > 0) & (picks == 1)
    dest = jnp.where(copied, host, ids)
    dest_row = as_row(dest)
    earlier = (dest == dest_row) & (iota((rows, rows), 1) < iota((rows, rows), 0))
    rank = jnp.sum(earlier.astype(jnp.int32), axis=1, keepdims=True)
    at_dest = iota((rows, n_dev), 1) == dest
    limit = jnp.sum(jnp.where(at_dest, cap_ref[...], 0), axis=1, keepdims=True)
    slot = jnp.where(rank < limit, (jnp.where(copied, CAP, 0) + rank) * n_dev + ids, -1)
    slot_ref[...] = slot
    pick = ones(iota((SLOTS * n_dev, rows), 0) == as_row(slot))
    owner = ones(iota((rows, toks), 0) // top == iota((rows, toks), 1))
    grad = (column(gate_ref[...]) * dot(owner, cot_ref[...], 1, 0)).astype(BF)
    pack(rows_ref, flat_ref, dot(pick, grad, 1, 0), dot(pick, act_ref[...], 1, 0))
    sent_ref[...] = rows_ref[...].astype(BF)


def backward(here_ref, got_ref, *refs):
    w_refs, (mine_ref, theirs_ref, grad_ref, rows_ref, flat_ref) = refs[:-5], refs[-5:]
    feats, hidden = grad_ref.shape[1], mine_ref.shape[1]
    rows_ref[...] = got_ref[...].astype(F32)
    grad, acts = unpack(rows_ref, flat_ref, feats, hidden)
    acts = acts.T.astype(BF)
    mine_ref[NY] = acts
    theirs_ref[NY] = acts
    grad = grad.astype(BF)
    grad_ref[...] = grad
    for step in range(NY):
        at = chip(here_ref[0], step)
        mine_ref[at] = dot(w_refs[2 * step][...], grad, 1, 1).astype(BF)
        theirs_ref[at] = dot(w_refs[2 * step + 1][...], grad, 1, 1).astype(BF)


def add_cores(mine_ref, theirs_ref, out_ref):
    for y in range(NY):
        out_ref[y, 0] = mine_ref[NY]
        out_ref[y, 1] = theirs_ref[NY]
        out_ref[y, 2] = (mine_ref[y].astype(F32) + theirs_ref[y].astype(F32)).astype(BF)


def forward(here_ref, all_ref, *refs):
    w_refs, (sent_ref, rows_ref, flat_ref) = refs[:-3], refs[-3:]
    total = None
    for step in range(NY):
        at = chip(here_ref[0], step)
        for other in range(2):
            part = dot(all_ref[at, other], w_refs[2 * step + other][...], 0, 0)
            total = part if total is None else total + part
    back = sum(all_ref[y, 2].astype(F32) for y in range(NY))
    pack(rows_ref, flat_ref, total, back.T)
    sent_ref[...] = rows_ref[...].astype(BF)


def weights_back(here_ref, all_ref, grad_ref, *outs):
    grad = grad_ref[...]
    for step in range(NY):
        at = chip(here_ref[0], step)
        for other in range(2):
            outs[2 * step + other][...] = dot(all_ref[at, other], grad, 1, 0).astype(BF)


def collect(got_ref, slot_ref, gate_ref, act_ref, mixed_ref, back_ref, gate_out_ref, rows_ref, flat_ref):
    top, toks = gate_ref.shape
    rows, hidden = back_ref.shape
    feats = mixed_ref.shape[1]
    rows_ref[...] = got_ref[...].astype(F32)
    outs, backs = unpack(rows_ref, flat_ref, feats, hidden)
    gate = column(gate_ref[...])
    pick = ones(iota((rows, outs.shape[0]), 1) == slot_ref[...])
    row_out = dot(pick, outs.astype(BF), 1, 0) * gate
    mixed_ref[...] = jnp.sum(row_out.reshape(toks, top, feats), axis=1).astype(BF)
    back = dot(pick, backs.astype(BF), 1, 0)
    back_ref[...] = back.astype(BF)
    gate_back = jnp.sum(back * act_ref[...].astype(F32), axis=1, keepdims=True) / gate
    at_tok = iota((rows, toks), 0) // top == iota((rows, toks), 1)
    spread = jnp.where(at_tok, gate_back, 0.0)
    gate_out_ref[...] = jnp.zeros_like(gate_out_ref)
    part = jnp.sum(spread.reshape(toks, top, toks), axis=0)
    for i in range(2 * NY):
        gate_out_ref[i, :, :toks] = part


def on_device(acts, w_down, gates, cotangent, expert_ids, replica_pick, placement, group_cap):
    n_dev = lax.axis_size("expert")
    toks, top, hidden = acts.shape
    feats = cotangent.shape[1]
    rows, slots = toks * top, SLOTS * n_dev
    _, narrow, per_peer = payload_rows(feats, hidden)
    payload = shape((n_dev * per_peer, LANES))
    scratch = [
        pltpu.VMEM((n_dev * per_peer, LANES), F32),
        pltpu.VMEM((n_dev, narrow * LANES), F32),
    ]
    here = lax.axis_index("dp").astype(jnp.int32).reshape(1)
    gates_t = gates.T
    pieces_shape = [shape((hidden, feats))] * (2 * NY)

    cuts = call(cut_weights, pieces_shape, [SM, VM], moved=3 << 20)(here, w_down[0])
    weights = [None] * (2 * NY)
    for step in range(NY):
        for other in range(2):
            piece = cuts[2 * step + other]
            if step or other:
                piece = send(piece, step, other)
            weights[2 * ((NY - step) % NY) + other] = piece

    inputs = (
        expert_ids.T, replica_pick.T, placement.T, group_cap.reshape(1, n_dev),
        acts.reshape(rows, hidden), cotangent, gates_t,
    )
    sent, slot = call(
        dispatch,
        [payload, shape((rows, 1), jnp.int32)],
        [pl.BlockSpec(memory_space=pltpu.HBM)] * len(inputs),
        scratch=[pltpu.VMEM(x.shape, x.dtype) for x in inputs]
        + scratch
        + [pltpu.SemaphoreType.DMA((len(inputs),))],
        vmem=63 << 20,
    )(*inputs)

    def exchange(value):
        value = value.reshape(n_dev, per_peer // TILE, TILE, LANES)
        return lax.all_to_all(value, "expert", 0, 0, tiled=True).reshape(payload.shape)

    got = exchange(sent)
    stack = shape((NY + 1, hidden, slots))
    flops = 2 * slots * feats * hidden * 2 * NY
    mine, theirs, grad = call(
        backward,
        [stack, stack, shape((slots, feats))],
        [SM] + [VM] * (1 + 2 * NY),
        flops=flops,
        scratch=scratch,
    )(here, got, *weights)
    theirs = send(theirs, 0, 1)
    shared = call(add_cores, shape((NY, 3, hidden, slots)), [VM] * 2)(mine, theirs)
    shared = exchange_y(shared)
    returned = call(forward, payload, [SM] + [VM] * (1 + 2 * NY), flops=flops, scratch=scratch)(
        here, shared, *weights
    )
    home = exchange(returned)

    pieces = call(weights_back, pieces_shape, [SM] + [VM] * 2, flops=flops)(here, shared, grad)
    joined = []
    for step in range(NY):
        for other in range(2):
            piece = pieces[2 * step + other]
            joined.append(send(piece, step, other) if step or other else piece)
    weight_grad = call(
        join_gradient, shape((hidden, 2 * NY * feats)), [SM] + [VM] * (2 * NY), moved=3 << 20
    )(here, *joined)

    home, weight_grad = lax.optimization_barrier((home, weight_grad))
    combined, back_rows, gate_parts = call(
        collect,
        [shape((toks, feats)), shape((rows, hidden)), shape((2 * NY, top, LANES), F32)],
        [VM] * 4,
        scratch=scratch,
    )(home, slot, gates_t, inputs[4])
    gate_parts = lax.all_to_all(gate_parts, "dp", 0, 0, tiled=True)
    gate_grad = jnp.sum(gate_parts, axis=0)[:, :toks].T
    return combined, back_rows.reshape(toks, top, hidden), weight_grad[None], gate_grad


def solution(mesh):
    return jax.shard_map(
        on_device,
        mesh=mesh,
        in_specs=(
            P("expert", None, "dp"),
            P("expert", "dp", None),
            P("expert", None),
            P("expert", "dp"),
            P("expert", None),
            P("expert", None),
            P(),
            P(),
        ),
        out_specs=(
            P("expert", "dp"),
            P("expert", None, "dp"),
            P("expert", "dp", None),
            P("expert", None),
        ),
        check_vma=False,
    )
```

```python
import functools

import jax
import jax.numpy as jnp
from jax import lax
from jax.experimental import pallas as pl
from jax.experimental.pallas import tpu as pltpu
from jax.sharding import PartitionSpec as P

CAP = 3
SLOTS = 2 * CAP
LANES = 128
TILE = 4
NY = 4
BF = jnp.bfloat16
F32 = jnp.float32
VM = pl.BlockSpec(memory_space=pltpu.VMEM)
SM = pl.BlockSpec(memory_space=pltpu.SMEM)


def call(kernel, outs, specs, flops=0, moved=1 << 20, scratch=(), vmem=40 << 20):
    return pl.pallas_call(
        kernel,
        out_shape=outs,
        in_specs=specs,
        out_specs=jax.tree.map(lambda _: VM, outs),
        scratch_shapes=list(scratch),
        compiler_params=pltpu.CompilerParams(vmem_limit_bytes=vmem),
        cost_estimate=pl.CostEstimate(flops=flops, bytes_accessed=moved, transcendentals=0),
    )


def dot(a, b, ca, cb):
    return lax.dot_general(a, b, (((ca,), (cb,)), ((), ())), preferred_element_type=F32)


def shape(dims, dtype=BF):
    return jax.ShapeDtypeStruct(dims, dtype)


def ones(mask):
    return mask.astype(F32).astype(BF)


def iota(dims, axis):
    return lax.broadcasted_iota(jnp.int32, dims, axis)


def payload_rows(feats, hidden):
    wide = SLOTS * feats // LANES
    narrow = -(-SLOTS * hidden // LANES)
    return wide, narrow, -(-(wide + narrow) // TILE) * TILE


def send(value, step, other):
    pairs = [(i, ((i // 2 + step) % NY) * 2 + ((i % 2) ^ other)) for i in range(2 * NY)]
    return lax.ppermute(value, "dp", pairs)


def exchange_y(value):
    groups = [[2 * y + core for y in range(NY)] for core in range(2)]
    return lax.all_to_all(value, "dp", 0, 0, axis_index_groups=groups, tiled=True)


def chip(here, step):
    return lax.rem(here // 2 + step, NY)


def chip_columns(here, step, width):
    return pl.ds(pl.multiple_of(chip(here, step) * width, width), width)


def core_columns(here, other, width):
    core = lax.rem(lax.rem(here, 2) + other, 2)
    return pl.ds(pl.multiple_of(core * width, width), width)


def cut_weights(here_ref, w_ref, *outs):
    width = outs[0].shape[1]
    for step in range(NY):
        outs[step][...] = w_ref[:, chip_columns(here_ref[0], step, width)]


def join_gradient(here_ref, *refs):
    parts, out_ref = refs[:-1], refs[-1]
    width = parts[0].shape[1]
    for step in range(NY):
        columns = chip_columns(here_ref[0], (NY - step) % NY, width)
        out_ref[:, columns] = parts[step][...]


def column(stored):
    top, toks = stored.shape
    spread = jnp.broadcast_to(stored[None], (toks, top, toks)).reshape(toks * top, toks)
    mine = iota(spread.shape, 0) // top == iota(spread.shape, 1)
    return jnp.sum(jnp.where(mine, spread, jnp.zeros_like(spread)), axis=1, keepdims=True)


def as_row(col):
    n = col.shape[0]
    diagonal = iota((n, n), 0) == iota((n, n), 1)
    return jnp.sum(jnp.where(diagonal, col, jnp.zeros_like(col)), axis=0, keepdims=True)


def pack(rows_ref, flat_ref, wide_vals, narrow_vals):
    n_dev = flat_ref.shape[0]
    feats, hidden = wide_vals.shape[1], narrow_vals.shape[1]
    wide, narrow, rows = payload_rows(feats, hidden)
    each = feats // LANES
    for j in range(SLOTS):
        part = slice(j * n_dev, (j + 1) * n_dev)
        for i in range(each):
            block = wide_vals[part, i * LANES : (i + 1) * LANES]
            rows_ref[pl.ds(j * each + i, n_dev, stride=rows), :] = block
        flat_ref[:, j * hidden : (j + 1) * hidden] = narrow_vals[part]
    for i in range(rows - wide):
        block = jnp.zeros((n_dev, LANES), F32)
        if i < narrow:
            block = flat_ref[:, i * LANES : (i + 1) * LANES]
        rows_ref[pl.ds(wide + i, n_dev, stride=rows), :] = block


def unpack(rows_ref, flat_ref, feats, hidden):
    n_dev = flat_ref.shape[0]
    wide, narrow, rows = payload_rows(feats, hidden)
    each = feats // LANES
    wide_vals = jnp.concatenate(
        [
            jnp.concatenate(
                [rows_ref[pl.ds(j * each + i, n_dev, stride=rows), :] for i in range(each)], axis=1
            )
            for j in range(SLOTS)
        ],
        axis=0,
    )
    for i in range(narrow):
        block = rows_ref[pl.ds(wide + i, n_dev, stride=rows), :]
        flat_ref[:, i * LANES : (i + 1) * LANES] = block
    narrow_vals = jnp.concatenate(
        [flat_ref[:, j * hidden : (j + 1) * hidden] for j in range(SLOTS)], axis=0
    )
    return wide_vals, narrow_vals


def dispatch(
    ids_hbm, picks_hbm, place_hbm, cap_hbm, act_hbm, cot_hbm, gate_hbm, sent_ref, slot_ref,
    ids_ref, picks_ref, place_ref, cap_ref, act_ref, cot_ref, gate_ref, rows_ref, flat_ref, sems,
):
    sources = (ids_hbm, picks_hbm, place_hbm, cap_hbm, act_hbm, cot_hbm, gate_hbm)
    targets = (ids_ref, picks_ref, place_ref, cap_ref, act_ref, cot_ref, gate_ref)
    copies = [
        pltpu.make_async_copy(source, target, sems.at[i])
        for i, (source, target) in enumerate(zip(sources, targets))
    ]
    for copy in copies:
        copy.start()
    for copy in copies:
        copy.wait()
    n_dev = cap_ref.shape[1]
    rows, hidden = act_ref.shape
    toks, feats = cot_ref.shape
    top = rows // toks
    ids, picks = column(ids_ref[...]), column(picks_ref[...])
    match = (place_ref[0:1, :] == ids).astype(jnp.int32)
    has = jnp.sum(match, axis=1, keepdims=True)
    host = jnp.sum(match * place_ref[1:2, :], axis=1, keepdims=True)
    copied = (has > 0) & (picks == 1)
    dest = jnp.where(copied, host, ids)
    dest_row = as_row(dest)
    earlier = (dest == dest_row) & (iota((rows, rows), 1) < iota((rows, rows), 0))
    rank = jnp.sum(earlier.astype(jnp.int32), axis=1, keepdims=True)
    at_dest = iota((rows, n_dev), 1) == dest
    limit = jnp.sum(jnp.where(at_dest, cap_ref[...], 0), axis=1, keepdims=True)
    slot = jnp.where(rank < limit, (jnp.where(copied, CAP, 0) + rank) * n_dev + ids, -1)
    slot_ref[...] = slot
    pick = ones(iota((SLOTS * n_dev, rows), 0) == as_row(slot))
    owner = ones(iota((rows, toks), 0) // top == iota((rows, toks), 1))
    grad = (column(gate_ref[...]) * dot(owner, cot_ref[...], 1, 0)).astype(BF)
    pack(rows_ref, flat_ref, dot(pick, grad, 1, 0), dot(pick, act_ref[...], 1, 0))
    sent_ref[...] = rows_ref[...].astype(BF)


def arrive(got_ref, grad_ref, act_ref, rows_ref, flat_ref):
    rows_ref[...] = got_ref[...].astype(F32)
    grad, acts = unpack(rows_ref, flat_ref, grad_ref.shape[1], act_ref.shape[0])
    grad_ref[...] = grad.astype(BF)
    act_ref[...] = acts.T.astype(BF)


def backward(here_ref, act_ref, near_ref, far_ref, *refs):
    w_refs, out_ref = refs[:-1], refs[-1]
    here, feats = here_ref[0], near_ref.shape[1]
    near, far = core_columns(here, 0, feats), core_columns(here, 1, feats)
    for step in range(NY):
        at, w_ref = chip(here, step), w_refs[step]
        part = dot(w_ref[:, near], near_ref[...], 1, 1) + dot(w_ref[:, far], far_ref[...], 1, 1)
        out_ref[at, 0] = act_ref[...]
        out_ref[at, 1] = part.astype(BF)


def forward(other, here_ref, all_ref, *refs):
    w_refs, out_ref = refs[:-1], refs[-1]
    here = here_ref[0]
    columns = core_columns(here, other, out_ref.shape[1])
    total = None
    for step in range(NY):
        part = dot(all_ref[chip(here, step), 0], w_refs[step][:, columns], 0, 0)
        total = part if total is None else total + part
    out_ref[...] = total.astype(out_ref.dtype)


def leave(all_ref, own_ref, swapped_ref, sent_ref, rows_ref, flat_ref):
    back = sum(all_ref[y, 1].astype(F32) for y in range(NY))
    pack(rows_ref, flat_ref, own_ref[...] + swapped_ref[...].astype(F32), back.T)
    sent_ref[...] = rows_ref[...].astype(BF)


def weights_back(here_ref, all_ref, near_ref, far_ref, *outs):
    here, feats = here_ref[0], near_ref.shape[1]
    near, far = core_columns(here, 0, feats), core_columns(here, 1, feats)
    for step in range(NY):
        acts = all_ref[chip(here, step), 0]
        outs[step][:, near] = dot(acts, near_ref[...], 1, 0).astype(BF)
        outs[step][:, far] = dot(acts, far_ref[...], 1, 0).astype(BF)


def collect(got_ref, slot_ref, gate_ref, act_ref, mixed_ref, back_ref, gate_out_ref, rows_ref, flat_ref):
    top, toks = gate_ref.shape
    rows, hidden = back_ref.shape
    feats = mixed_ref.shape[1]
    rows_ref[...] = got_ref[...].astype(F32)
    outs, backs = unpack(rows_ref, flat_ref, feats, hidden)
    gate = column(gate_ref[...])
    pick = ones(iota((rows, outs.shape[0]), 1) == slot_ref[...])
    row_out = dot(pick, outs.astype(BF), 1, 0) * gate
    mixed_ref[...] = jnp.sum(row_out.reshape(toks, top, feats), axis=1).astype(BF)
    back = dot(pick, backs.astype(BF), 1, 0)
    back_ref[...] = back.astype(BF)
    gate_back = jnp.sum(back * act_ref[...].astype(F32), axis=1, keepdims=True) / gate
    at_tok = iota((rows, toks), 0) // top == iota((rows, toks), 1)
    spread = jnp.where(at_tok, gate_back, 0.0)
    gate_out_ref[...] = jnp.zeros_like(gate_out_ref)
    part = jnp.sum(spread.reshape(toks, top, toks), axis=0)
    for i in range(2 * NY):
        gate_out_ref[i, :, :toks] = part


def on_device(acts, w_down, gates, cotangent, expert_ids, replica_pick, placement, group_cap):
    n_dev = lax.axis_size("expert")
    toks, top, hidden = acts.shape
    feats = cotangent.shape[1]
    rows, slots = toks * top, SLOTS * n_dev
    _, narrow, per_peer = payload_rows(feats, hidden)
    payload = shape((n_dev * per_peer, LANES))
    scratch = [
        pltpu.VMEM((n_dev * per_peer, LANES), F32),
        pltpu.VMEM((n_dev, narrow * LANES), F32),
    ]
    here = lax.axis_index("dp").astype(jnp.int32).reshape(1)
    gates_t = gates.T
    pieces_shape = [shape((hidden, 2 * feats))] * NY

    cuts = call(cut_weights, pieces_shape, [SM, VM], moved=3 << 20)(here, w_down[0])
    weights = [cuts[0]] + [send(cuts[NY - step], NY - step, 0) for step in range(1, NY)]

    inputs = (
        expert_ids.T, replica_pick.T, placement.T, group_cap.reshape(1, n_dev),
        acts.reshape(rows, hidden), cotangent, gates_t,
    )
    sent, slot = call(
        dispatch,
        [payload, shape((rows, 1), jnp.int32)],
        [pl.BlockSpec(memory_space=pltpu.HBM)] * len(inputs),
        scratch=[pltpu.VMEM(x.shape, x.dtype) for x in inputs]
        + scratch
        + [pltpu.SemaphoreType.DMA((len(inputs),))],
        vmem=63 << 20,
    )(*inputs)

    def exchange(value):
        value = value.reshape(n_dev, per_peer // TILE, TILE, LANES)
        return lax.all_to_all(value, "expert", 0, 0, tiled=True).reshape(payload.shape)

    got = exchange(sent)
    flops = 2 * slots * feats * hidden * 2 * NY
    grad, own_act = call(
        arrive, [shape((slots, feats)), shape((hidden, slots))], [VM], scratch=scratch
    )(got)
    far_grad = send(grad, 0, 1)
    shared = call(
        backward, shape((NY, 2, hidden, slots)), [SM] + [VM] * (3 + NY), flops=flops
    )(here, own_act, grad, far_grad, *weights)
    shared = exchange_y(shared)

    def part(other, dtype):
        return call(
            functools.partial(forward, other),
            shape((slots, feats), dtype),
            [SM] + [VM] * (1 + NY),
            flops=flops // 2,
        )(here, shared, *weights)

    swapped = send(part(1, BF), 0, 1)
    returned = call(leave, payload, [VM] * 3, scratch=scratch)(shared, part(0, F32), swapped)
    home = exchange(returned)

    pieces = call(weights_back, pieces_shape, [SM] + [VM] * 3, flops=flops)(
        here, shared, grad, far_grad
    )
    joined = [pieces[0]] + [send(pieces[step], step, 0) for step in range(1, NY)]
    weight_grad = call(
        join_gradient, shape((hidden, 2 * NY * feats)), [SM] + [VM] * NY, moved=3 << 20
    )(here, *joined)

    home, weight_grad = lax.optimization_barrier((home, weight_grad))
    combined, back_rows, gate_parts = call(
        collect,
        [shape((toks, feats)), shape((rows, hidden)), shape((2 * NY, top, LANES), F32)],
        [VM] * 4,
        scratch=scratch,
    )(home, slot, gates_t, inputs[4])
    gate_parts = lax.all_to_all(gate_parts, "dp", 0, 0, tiled=True)
    gate_grad = jnp.sum(gate_parts, axis=0)[:, :toks].T
    return combined, back_rows.reshape(toks, top, hidden), weight_grad[None], gate_grad


def solution(mesh):
    return jax.shard_map(
        on_device,
        mesh=mesh,
        in_specs=(
            P("expert", None, "dp"),
            P("expert", "dp", None),
            P("expert", None),
            P("expert", "dp"),
            P("expert", None),
            P("expert", None),
            P(),
            P(),
        ),
        out_specs=(
            P("expert", "dp"),
            P("expert", None, "dp"),
            P("expert", "dp", None),
            P("expert", None),
        ),
        check_vma=False,
    )
```

```python
import functools

import jax
import jax.numpy as jnp
from jax import lax
from jax.experimental import pallas as pl
from jax.experimental.pallas import tpu as pltpu
from jax.sharding import PartitionSpec as P

CAP = 3
SLOTS = 2 * CAP
LANES = 128
TILE = 4
NY = 4
BF = jnp.bfloat16
F32 = jnp.float32
VM = pl.BlockSpec(memory_space=pltpu.VMEM)
SM = pl.BlockSpec(memory_space=pltpu.SMEM)


def call(kernel, outs, specs, flops=0, moved=1 << 20, scratch=(), vmem=16 << 20):
    return pl.pallas_call(
        kernel,
        out_shape=outs,
        in_specs=specs,
        out_specs=jax.tree.map(lambda _: VM, outs),
        scratch_shapes=list(scratch),
        compiler_params=pltpu.CompilerParams(vmem_limit_bytes=vmem),
        cost_estimate=pl.CostEstimate(flops=flops, bytes_accessed=moved, transcendentals=0),
    )


def dot(a, b, ca, cb):
    return lax.dot_general(a, b, (((ca,), (cb,)), ((), ())), preferred_element_type=F32)


def shape(dims, dtype=BF):
    return jax.ShapeDtypeStruct(dims, dtype)


def ones(mask):
    return mask.astype(F32).astype(BF)


def iota(dims, axis):
    return lax.broadcasted_iota(jnp.int32, dims, axis)


def payload_rows(feats, hidden):
    wide = SLOTS * feats // LANES
    narrow = -(-SLOTS * hidden // LANES)
    return wide, narrow, -(-(wide + narrow) // TILE) * TILE


def send(value, step, other):
    pairs = [(i, ((i // 2 + step) % NY) * 2 + ((i % 2) ^ other)) for i in range(2 * NY)]
    return lax.ppermute(value, "dp", pairs)


def exchange_y(value):
    groups = [[2 * y + core for y in range(NY)] for core in range(2)]
    return lax.all_to_all(value, "dp", 0, 0, axis_index_groups=groups, tiled=True)


def chip(here, step):
    return lax.rem(here // 2 + step, NY)


def chip_columns(here, step, width):
    return pl.ds(pl.multiple_of(chip(here, step) * width, width), width)


def core_columns(here, other, width):
    core = lax.rem(lax.rem(here, 2) + other, 2)
    return pl.ds(pl.multiple_of(core * width, width), width)


def cut_weights(here_ref, w_ref, *outs):
    width = outs[0].shape[1]
    for step in range(NY):
        outs[step][...] = w_ref[:, chip_columns(here_ref[0], step, width)]


def join_gradient(here_ref, *refs):
    parts, out_ref = refs[:-1], refs[-1]
    width = parts[0].shape[1]
    for step in range(NY):
        columns = chip_columns(here_ref[0], (NY - step) % NY, width)
        out_ref[:, columns] = parts[step][...]


def column(stored):
    top, toks = stored.shape
    spread = jnp.broadcast_to(stored[None], (toks, top, toks)).reshape(toks * top, toks)
    mine = iota(spread.shape, 0) // top == iota(spread.shape, 1)
    return jnp.sum(jnp.where(mine, spread, jnp.zeros_like(spread)), axis=1, keepdims=True)


def as_row(col):
    n = col.shape[0]
    diagonal = iota((n, n), 0) == iota((n, n), 1)
    return jnp.sum(jnp.where(diagonal, col, jnp.zeros_like(col)), axis=0, keepdims=True)


def pack(rows_ref, flat_ref, wide_vals, narrow_vals):
    n_dev = flat_ref.shape[0]
    feats, hidden = wide_vals.shape[1], narrow_vals.shape[1]
    wide, narrow, rows = payload_rows(feats, hidden)
    each = feats // LANES
    for j in range(SLOTS):
        part = slice(j * n_dev, (j + 1) * n_dev)
        for i in range(each):
            block = wide_vals[part, i * LANES : (i + 1) * LANES]
            rows_ref[pl.ds(j * each + i, n_dev, stride=rows), :] = block
        flat_ref[:, j * hidden : (j + 1) * hidden] = narrow_vals[part]
    for i in range(rows - wide):
        block = jnp.zeros((n_dev, LANES), F32)
        if i < narrow:
            block = flat_ref[:, i * LANES : (i + 1) * LANES]
        rows_ref[pl.ds(wide + i, n_dev, stride=rows), :] = block


def unpack(rows_ref, flat_ref, feats, hidden):
    n_dev = flat_ref.shape[0]
    wide, narrow, rows = payload_rows(feats, hidden)
    each = feats // LANES
    wide_vals = jnp.concatenate(
        [
            jnp.concatenate(
                [rows_ref[pl.ds(j * each + i, n_dev, stride=rows), :] for i in range(each)], axis=1
            )
            for j in range(SLOTS)
        ],
        axis=0,
    )
    for i in range(narrow):
        block = rows_ref[pl.ds(wide + i, n_dev, stride=rows), :]
        flat_ref[:, i * LANES : (i + 1) * LANES] = block
    narrow_vals = jnp.concatenate(
        [flat_ref[:, j * hidden : (j + 1) * hidden] for j in range(SLOTS)], axis=0
    )
    return wide_vals, narrow_vals


def dispatch(
    ids_hbm, picks_hbm, place_hbm, cap_hbm, act_hbm, cot_hbm, gate_hbm, sent_ref, slot_ref,
    ids_ref, picks_ref, place_ref, cap_ref, act_ref, cot_ref, gate_ref, rows_ref, flat_ref, sems,
):
    sources = (ids_hbm, picks_hbm, place_hbm, cap_hbm, act_hbm, cot_hbm, gate_hbm)
    targets = (ids_ref, picks_ref, place_ref, cap_ref, act_ref, cot_ref, gate_ref)
    copies = [
        pltpu.make_async_copy(source, target, sems.at[i])
        for i, (source, target) in enumerate(zip(sources, targets))
    ]
    for copy in copies:
        copy.start()
    for copy in copies[:4]:
        copy.wait()
    n_dev = cap_ref.shape[1]
    rows, hidden = act_ref.shape
    toks, feats = cot_ref.shape
    top = rows // toks
    ids, picks = column(ids_ref[...]), column(picks_ref[...])
    match = (place_ref[0:1, :] == ids).astype(jnp.int32)
    has = jnp.sum(match, axis=1, keepdims=True)
    host = jnp.sum(match * place_ref[1:2, :], axis=1, keepdims=True)
    copied = (has > 0) & (picks == 1)
    dest = jnp.where(copied, host, ids)
    dest_row = as_row(dest)
    earlier = (dest == dest_row) & (iota((rows, rows), 1) < iota((rows, rows), 0))
    rank = jnp.sum(earlier.astype(jnp.int32), axis=1, keepdims=True)
    at_dest = iota((rows, n_dev), 1) == dest
    limit = jnp.sum(jnp.where(at_dest, cap_ref[...], 0), axis=1, keepdims=True)
    slot = jnp.where(rank < limit, (jnp.where(copied, CAP, 0) + rank) * n_dev + ids, -1)
    slot_ref[...] = slot
    pick = ones(iota((SLOTS * n_dev, rows), 0) == as_row(slot))
    owner = ones(iota((rows, toks), 0) // top == iota((rows, toks), 1))
    for copy in copies[4:]:
        copy.wait()
    grad = (column(gate_ref[...]) * dot(owner, cot_ref[...], 1, 0)).astype(BF)
    pack(rows_ref, flat_ref, dot(pick, grad, 1, 0), dot(pick, act_ref[...], 1, 0))
    sent_ref[...] = rows_ref[...].astype(BF)


def arrive(got_ref, grad_ref, act_ref, rows_ref, flat_ref):
    rows_ref[...] = got_ref[...].astype(F32)
    grad, acts = unpack(rows_ref, flat_ref, grad_ref.shape[1], act_ref.shape[0])
    grad_ref[...] = grad.astype(BF)
    act_ref[...] = acts.T.astype(BF)


def backward(here_ref, near_ref, far_ref, *refs):
    w_refs, out_ref = refs[:-1], refs[-1]
    here, feats = here_ref[0], near_ref.shape[1]
    near, far = core_columns(here, 0, feats), core_columns(here, 1, feats)
    for step in range(NY):
        w_ref = w_refs[step]
        part = dot(w_ref[:, near], near_ref[...], 1, 1) + dot(w_ref[:, far], far_ref[...], 1, 1)
        out_ref[chip(here, step)] = part.astype(BF)


def forward(other, here_ref, *refs):
    act_refs, w_refs, out_ref = refs[:NY], refs[NY:-1], refs[-1]
    columns = core_columns(here_ref[0], other, out_ref.shape[1])
    total = None
    for act_ref, w_ref in zip(act_refs, w_refs):
        part = dot(act_ref[...], w_ref[:, columns], 0, 0)
        total = part if total is None else total + part
    out_ref[...] = total.astype(out_ref.dtype)


def leave(back_ref, own_ref, swapped_ref, sent_ref, rows_ref, flat_ref):
    back = sum(back_ref[y].astype(F32) for y in range(NY))
    pack(rows_ref, flat_ref, own_ref[...] + swapped_ref[...].astype(F32), back.T)
    sent_ref[...] = rows_ref[...].astype(BF)


def weights_back(here_ref, near_ref, far_ref, *refs):
    act_refs, outs = refs[:NY], refs[NY:]
    here, feats = here_ref[0], near_ref.shape[1]
    near, far = core_columns(here, 0, feats), core_columns(here, 1, feats)
    for act_ref, out_ref in zip(act_refs, outs):
        out_ref[:, near] = dot(act_ref[...], near_ref[...], 1, 0).astype(BF)
        out_ref[:, far] = dot(act_ref[...], far_ref[...], 1, 0).astype(BF)


def collect(got_ref, slot_ref, gate_ref, act_ref, mixed_ref, back_ref, gate_out_ref, rows_ref, flat_ref):
    top, toks = gate_ref.shape
    rows, hidden = back_ref.shape
    feats = mixed_ref.shape[1]
    rows_ref[...] = got_ref[...].astype(F32)
    outs, backs = unpack(rows_ref, flat_ref, feats, hidden)
    gate = column(gate_ref[...])
    pick = ones(iota((rows, outs.shape[0]), 1) == slot_ref[...])
    row_out = dot(pick, outs.astype(BF), 1, 0) * gate
    mixed_ref[...] = jnp.sum(row_out.reshape(toks, top, feats), axis=1).astype(BF)
    back = dot(pick, backs.astype(BF), 1, 0)
    back_ref[...] = back.astype(BF)
    gate_back = jnp.sum(back * act_ref[...].astype(F32), axis=1, keepdims=True) / gate
    at_tok = iota((rows, toks), 0) // top == iota((rows, toks), 1)
    spread = jnp.where(at_tok, gate_back, 0.0)
    gate_out_ref[...] = jnp.zeros_like(gate_out_ref)
    part = jnp.sum(spread.reshape(toks, top, toks), axis=0)
    for i in range(2 * NY):
        gate_out_ref[i, :, :toks] = part


def on_device(acts, w_down, gates, cotangent, expert_ids, replica_pick, placement, group_cap):
    n_dev = lax.axis_size("expert")
    toks, top, hidden = acts.shape
    feats = cotangent.shape[1]
    rows, slots = toks * top, SLOTS * n_dev
    _, narrow, per_peer = payload_rows(feats, hidden)
    payload = shape((n_dev * per_peer, LANES))
    scratch = [
        pltpu.VMEM((n_dev * per_peer, LANES), F32),
        pltpu.VMEM((n_dev, narrow * LANES), F32),
    ]
    here = lax.axis_index("dp").astype(jnp.int32).reshape(1)
    gates_t = gates.T
    pieces_shape = [shape((hidden, 2 * feats))] * NY

    cuts = call(cut_weights, pieces_shape, [SM, VM], moved=3 << 20)(here, w_down[0])
    weights = [cuts[0]] + [send(cuts[NY - step], NY - step, 0) for step in range(1, NY)]

    inputs = (
        expert_ids.T, replica_pick.T, placement.T, group_cap.reshape(1, n_dev),
        acts.reshape(rows, hidden), cotangent, gates_t,
    )
    sent, slot = call(
        dispatch,
        [payload, shape((rows, 1), jnp.int32)],
        [pl.BlockSpec(memory_space=pltpu.HBM)] * len(inputs),
        scratch=[pltpu.VMEM(x.shape, x.dtype) for x in inputs]
        + scratch
        + [pltpu.SemaphoreType.DMA((len(inputs),))],
        vmem=63 << 20,
    )(*inputs)

    def exchange(value):
        value = value.reshape(n_dev, per_peer // TILE, TILE, LANES)
        return lax.all_to_all(value, "expert", 0, 0, tiled=True).reshape(payload.shape)

    got = exchange(sent)
    flops = 2 * slots * feats * hidden * 2 * NY
    grad, own_act = call(
        arrive, [shape((slots, feats)), shape((hidden, slots))], [VM], scratch=scratch
    )(got)
    far_grad = send(grad, 0, 1)
    all_acts = [own_act] + [send(own_act, NY - step, 0) for step in range(1, NY)]
    back = call(backward, shape((NY, hidden, slots)), [SM] + [VM] * (2 + NY), flops=flops)(
        here, grad, far_grad, *weights
    )
    back = exchange_y(back)

    def part(other, dtype):
        return call(
            functools.partial(forward, other),
            shape((slots, feats), dtype),
            [SM] + [VM] * (2 * NY),
            flops=flops // 2,
        )(here, *all_acts, *weights)

    swapped = send(part(1, BF), 0, 1)
    returned = call(leave, payload, [VM] * 3, scratch=scratch)(back, part(0, F32), swapped)
    home = exchange(returned)

    pieces = call(weights_back, pieces_shape, [SM] + [VM] * (2 + NY), flops=flops)(
        here, grad, far_grad, *all_acts
    )
    joined = [pieces[0]] + [send(pieces[step], step, 0) for step in range(1, NY)]
    weight_grad = call(
        join_gradient, shape((hidden, 2 * NY * feats)), [SM] + [VM] * NY, moved=3 << 20
    )(here, *joined)

    home, weight_grad = lax.optimization_barrier((home, weight_grad))
    combined, back_rows, gate_parts = call(
        collect,
        [shape((toks, feats)), shape((rows, hidden)), shape((2 * NY, top, LANES), F32)],
        [VM] * 4,
        scratch=scratch,
    )(home, slot, gates_t, inputs[4])
    gate_parts = lax.all_to_all(gate_parts, "dp", 0, 0, tiled=True)
    gate_grad = jnp.sum(gate_parts, axis=0)[:, :toks].T
    return combined, back_rows.reshape(toks, top, hidden), weight_grad[None], gate_grad


def solution(mesh):
    return jax.shard_map(
        on_device,
        mesh=mesh,
        in_specs=(
            P("expert", None, "dp"),
            P("expert", "dp", None),
            P("expert", None),
            P("expert", "dp"),
            P("expert", None),
            P("expert", None),
            P(),
            P(),
        ),
        out_specs=(
            P("expert", "dp"),
            P("expert", None, "dp"),
            P("expert", "dp", None),
            P("expert", None),
        ),
        check_vma=False,
    )
```

```python
import functools

import jax
import jax.numpy as jnp
from jax import lax
from jax.experimental import pallas as pl
from jax.experimental.pallas import tpu as pltpu
from jax.sharding import PartitionSpec as P

CAP = 3
SLOTS = 2 * CAP
LANES = 128
TILE = 4
NY = 4
EXTRA = 16
BF = jnp.bfloat16
F32 = jnp.float32
VM = pl.BlockSpec(memory_space=pltpu.VMEM)
SM = pl.BlockSpec(memory_space=pltpu.SMEM)


def call(kernel, outs, specs, flops=0, moved=1 << 20, scratch=(), vmem=16 << 20):
    return pl.pallas_call(
        kernel,
        out_shape=outs,
        in_specs=specs,
        out_specs=jax.tree.map(lambda _: VM, outs),
        scratch_shapes=list(scratch),
        compiler_params=pltpu.CompilerParams(vmem_limit_bytes=vmem),
        cost_estimate=pl.CostEstimate(flops=flops, bytes_accessed=moved, transcendentals=0),
    )


def dot(a, b, ca, cb):
    return lax.dot_general(a, b, (((ca,), (cb,)), ((), ())), preferred_element_type=F32)


def shape(dims, dtype=BF):
    return jax.ShapeDtypeStruct(dims, dtype)


def ones(mask):
    return mask.astype(F32).astype(BF)


def iota(dims, axis):
    return lax.broadcasted_iota(jnp.int32, dims, axis)


def payload_rows(feats, hidden):
    wide = SLOTS * feats // LANES
    narrow = -(-SLOTS * hidden // LANES)
    return wide, narrow, -(-(wide + narrow + 1) // TILE) * TILE


def send(value, step, other):
    pairs = [(i, ((i // 2 + step) % NY) * 2 + ((i % 2) ^ other)) for i in range(2 * NY)]
    return lax.ppermute(value, "dp", pairs)


def exchange_y(value):
    groups = [[2 * y + core for y in range(NY)] for core in range(2)]
    return lax.all_to_all(value, "dp", 0, 0, axis_index_groups=groups, tiled=True)


def chip(here, step):
    return lax.rem(here // 2 + step, NY)


def chip_columns(here, step, width):
    return pl.ds(pl.multiple_of(chip(here, step) * width, width), width)


def core_columns(here, other, width):
    core = lax.rem(lax.rem(here, 2) + other, 2)
    return pl.ds(pl.multiple_of(core * width, width), width)


def cut_weights(here_ref, w_ref, *outs):
    width = outs[0].shape[1]
    for step in range(NY):
        outs[step][...] = w_ref[:, chip_columns(here_ref[0], step, width)]


def join_gradient(here_ref, *refs):
    parts, out_ref = refs[:-1], refs[-1]
    width = parts[0].shape[1]
    for step in range(NY):
        columns = chip_columns(here_ref[0], (NY - step) % NY, width)
        out_ref[:, columns] = parts[step][...]


def column(stored):
    top, toks = stored.shape
    spread = jnp.broadcast_to(stored[None], (toks, top, toks)).reshape(toks * top, toks)
    mine = iota(spread.shape, 0) // top == iota(spread.shape, 1)
    return jnp.sum(jnp.where(mine, spread, jnp.zeros_like(spread)), axis=1, keepdims=True)


def as_row(col):
    n = col.shape[0]
    diagonal = iota((n, n), 0) == iota((n, n), 1)
    return jnp.sum(jnp.where(diagonal, col, jnp.zeros_like(col)), axis=0, keepdims=True)


def pack(rows_ref, flat_ref, wide_vals, narrow_vals, scalars=None):
    n_dev = flat_ref.shape[0]
    feats, hidden = wide_vals.shape[1], narrow_vals.shape[1]
    wide, narrow, rows = payload_rows(feats, hidden)
    each = feats // LANES
    for j in range(SLOTS):
        part = slice(j * n_dev, (j + 1) * n_dev)
        for i in range(each):
            block = wide_vals[part, i * LANES : (i + 1) * LANES]
            rows_ref[pl.ds(j * each + i, n_dev, stride=rows), :] = block
        flat_ref[:, j * hidden : (j + 1) * hidden] = narrow_vals[part]
    for i in range(rows - wide):
        block = jnp.zeros((n_dev, LANES), F32)
        if i < narrow:
            block = flat_ref[:, i * LANES : (i + 1) * LANES]
        rows_ref[pl.ds(wide + i, n_dev, stride=rows), :] = block
    if scalars is not None:
        for j in range(SLOTS):
            part = scalars[j * n_dev : (j + 1) * n_dev]
            flat_ref[:, j * EXTRA : (j + 1) * EXTRA] = part
        flat_ref[:, SLOTS * EXTRA : LANES] = jnp.zeros((n_dev, LANES - SLOTS * EXTRA), F32)
        rows_ref[pl.ds(wide + narrow, n_dev, stride=rows), :] = flat_ref[:, :LANES]


def unpack_scalars(rows_ref, n_dev, feats, hidden):
    wide, narrow, rows = payload_rows(feats, hidden)
    block = rows_ref[pl.ds(wide + narrow, n_dev, stride=rows), :]
    return jnp.concatenate([block[:, j * EXTRA : (j + 1) * EXTRA] for j in range(SLOTS)], axis=0)


def two_parts(row):
    high = row.astype(BF).astype(F32)
    at = iota((EXTRA, row.shape[1]), 0)
    return jnp.where(at == 0, high, jnp.where(at == 1, row - high, 0.0))


def unpack(rows_ref, flat_ref, feats, hidden):
    n_dev = flat_ref.shape[0]
    wide, narrow, rows = payload_rows(feats, hidden)
    each = feats // LANES
    wide_vals = jnp.concatenate(
        [
            jnp.concatenate(
                [rows_ref[pl.ds(j * each + i, n_dev, stride=rows), :] for i in range(each)], axis=1
            )
            for j in range(SLOTS)
        ],
        axis=0,
    )
    for i in range(narrow):
        block = rows_ref[pl.ds(wide + i, n_dev, stride=rows), :]
        flat_ref[:, i * LANES : (i + 1) * LANES] = block
    narrow_vals = jnp.concatenate(
        [flat_ref[:, j * hidden : (j + 1) * hidden] for j in range(SLOTS)], axis=0
    )
    return wide_vals, narrow_vals


def dispatch(
    ids_hbm, picks_hbm, place_hbm, cap_hbm, act_hbm, cot_hbm, gate_hbm, sent_ref, slot_ref,
    ids_ref, picks_ref, place_ref, cap_ref, act_ref, cot_ref, gate_ref, rows_ref, flat_ref, sems,
):
    sources = (ids_hbm, picks_hbm, place_hbm, cap_hbm, act_hbm, cot_hbm, gate_hbm)
    targets = (ids_ref, picks_ref, place_ref, cap_ref, act_ref, cot_ref, gate_ref)
    copies = [
        pltpu.make_async_copy(source, target, sems.at[i])
        for i, (source, target) in enumerate(zip(sources, targets))
    ]
    for copy in copies:
        copy.start()
    for copy in copies[:4]:
        copy.wait()
    n_dev = cap_ref.shape[1]
    rows, hidden = act_ref.shape
    toks, feats = cot_ref.shape
    top = rows // toks
    ids, picks = column(ids_ref[...]), column(picks_ref[...])
    match = (place_ref[0:1, :] == ids).astype(jnp.int32)
    has = jnp.sum(match, axis=1, keepdims=True)
    host = jnp.sum(match * place_ref[1:2, :], axis=1, keepdims=True)
    copied = (has > 0) & (picks == 1)
    dest = jnp.where(copied, host, ids)
    dest_row = as_row(dest)
    earlier = (dest == dest_row) & (iota((rows, rows), 1) < iota((rows, rows), 0))
    rank = jnp.sum(earlier.astype(jnp.int32), axis=1, keepdims=True)
    at_dest = iota((rows, n_dev), 1) == dest
    limit = jnp.sum(jnp.where(at_dest, cap_ref[...], 0), axis=1, keepdims=True)
    slot = jnp.where(rank < limit, (jnp.where(copied, CAP, 0) + rank) * n_dev + ids, -1)
    slot_ref[...] = slot
    pick = ones(iota((SLOTS * n_dev, rows), 0) == as_row(slot))
    owner = ones(iota((rows, toks), 0) // top == iota((rows, toks), 1))
    for copy in copies[4:]:
        copy.wait()
    grad = (column(gate_ref[...]) * dot(owner, cot_ref[...], 1, 0)).astype(BF)
    pack(rows_ref, flat_ref, dot(pick, grad, 1, 0), dot(pick, act_ref[...], 1, 0))
    sent_ref[...] = rows_ref[...].astype(BF)


def arrive(got_ref, grad_ref, act_ref, rows_ref, flat_ref):
    rows_ref[...] = got_ref[...].astype(F32)
    grad, acts = unpack(rows_ref, flat_ref, grad_ref.shape[1], act_ref.shape[1])
    grad_ref[...] = grad.astype(BF)
    acts = acts.T.astype(BF)
    for y in range(NY):
        act_ref[y] = acts


def seal(part_ref, act_ref, out_ref):
    hidden, slots = act_ref.shape[1:]
    gate = jnp.zeros((1, slots), F32)
    for y in range(NY):
        part = part_ref[y]
        products = act_ref[y].astype(F32) * part.astype(F32)
        gate = gate + jnp.sum(products, axis=0, keepdims=True)
        out_ref[y, :hidden] = part
    extra = two_parts(gate).astype(BF)
    for y in range(NY):
        out_ref[y, hidden:] = extra


def backward(here_ref, near_ref, far_ref, *refs):
    w_refs, out_ref = refs[:-1], refs[-1]
    here, feats = here_ref[0], near_ref.shape[1]
    near, far = core_columns(here, 0, feats), core_columns(here, 1, feats)
    for step in range(NY):
        w_ref = w_refs[step]
        part = dot(w_ref[:, near], near_ref[...], 1, 1) + dot(w_ref[:, far], far_ref[...], 1, 1)
        out_ref[chip(here, step)] = part.astype(BF)


def forward(other, here_ref, act_ref, *refs):
    w_refs, more, out_ref = refs[:NY], refs[NY:-1], refs[-1]
    here = here_ref[0]
    columns = core_columns(here, other, out_ref.shape[1])
    total = more[0][...].astype(F32) if more else None
    for step in range(NY):
        part = dot(act_ref[chip(here, step)], w_refs[step][:, columns], 0, 0)
        total = part if total is None else total + part
    out_ref[...] = total.astype(out_ref.dtype)


def leave(back_ref, wide_ref, sent_ref, rows_ref, flat_ref):
    back = sum(back_ref[y].astype(F32) for y in range(NY))
    hidden = back.shape[0] - EXTRA
    gate = jnp.sum(back[hidden:], axis=0, keepdims=True)
    pack(rows_ref, flat_ref, wide_ref[...], back[:hidden].T, two_parts(gate).T)
    sent_ref[...] = rows_ref[...].astype(BF)


def weights_back(here_ref, near_ref, far_ref, act_ref, *outs):
    here, feats = here_ref[0], near_ref.shape[1]
    near, far = core_columns(here, 0, feats), core_columns(here, 1, feats)
    for step in range(NY):
        acts = act_ref[chip(here, step)]
        outs[step][:, near] = dot(acts, near_ref[...], 1, 0).astype(BF)
        outs[step][:, far] = dot(acts, far_ref[...], 1, 0).astype(BF)


def collect(got_ref, slot_ref, gate_ref, mixed_ref, back_ref, gate_out_ref, rows_ref, flat_ref):
    top, toks = gate_ref.shape
    rows, hidden = back_ref.shape
    feats = mixed_ref.shape[1]
    rows_ref[...] = got_ref[...].astype(F32)
    outs, backs = unpack(rows_ref, flat_ref, feats, hidden)
    gate = column(gate_ref[...])
    pick = ones(iota((rows, outs.shape[0]), 1) == slot_ref[...])
    row_out = dot(pick, outs.astype(BF), 1, 0) * gate
    mixed_ref[...] = jnp.sum(row_out.reshape(toks, top, feats), axis=1).astype(BF)
    back = dot(pick, backs.astype(BF), 1, 0)
    back_ref[...] = back.astype(BF)
    scalars = unpack_scalars(rows_ref, flat_ref.shape[0], feats, hidden)
    gate_back = jnp.sum(dot(pick, scalars.astype(BF), 1, 0), axis=1, keepdims=True) / gate
    at_tok = iota((rows, toks), 0) // top == iota((rows, toks), 1)
    spread = jnp.where(at_tok, gate_back, 0.0)
    gate_out_ref[...] = jnp.sum(spread.reshape(toks, top, toks), axis=0)


def on_device(acts, w_down, gates, cotangent, expert_ids, replica_pick, placement, group_cap):
    n_dev = lax.axis_size("expert")
    toks, top, hidden = acts.shape
    feats = cotangent.shape[1]
    rows, slots = toks * top, SLOTS * n_dev
    _, narrow, per_peer = payload_rows(feats, hidden)
    payload = shape((n_dev * per_peer, LANES))
    scratch = [
        pltpu.VMEM((n_dev * per_peer, LANES), F32),
        pltpu.VMEM((n_dev, narrow * LANES), F32),
    ]
    here = lax.axis_index("dp").astype(jnp.int32).reshape(1)
    gates_t = gates.T
    pieces_shape = [shape((hidden, 2 * feats))] * NY

    cuts = call(cut_weights, pieces_shape, [SM, VM], moved=3 << 20)(here, w_down[0])
    weights = [cuts[0]] + [send(cuts[NY - step], NY - step, 0) for step in range(1, NY)]

    inputs = (
        expert_ids.T, replica_pick.T, placement.T, group_cap.reshape(1, n_dev),
        acts.reshape(rows, hidden), cotangent, gates_t,
    )
    sent, slot = call(
        dispatch,
        [payload, shape((rows, 1), jnp.int32)],
        [pl.BlockSpec(memory_space=pltpu.HBM)] * len(inputs),
        scratch=[pltpu.VMEM(x.shape, x.dtype) for x in inputs]
        + scratch
        + [pltpu.SemaphoreType.DMA((len(inputs),))],
        vmem=63 << 20,
    )(*inputs)

    def exchange(value):
        value = value.reshape(n_dev, per_peer // TILE, TILE, LANES)
        return lax.all_to_all(value, "expert", 0, 0, tiled=True).reshape(payload.shape)

    got = exchange(sent)
    flops = 2 * slots * feats * hidden * 2 * NY
    stack = shape((NY, hidden, slots))
    grad, own_act = call(arrive, [shape((slots, feats)), stack], [VM], scratch=scratch)(got)
    near_act = exchange_y(own_act)
    far_grad = send(grad, 0, 1)
    back = call(backward, stack, [SM] + [VM] * (2 + NY), flops=flops)(
        here, grad, far_grad, *weights
    )
    back = call(seal, shape((NY, hidden + EXTRA, slots)), [VM] * 2)(back, near_act)
    back = exchange_y(back)

    def part(other, dtype, *more):
        return call(
            functools.partial(forward, other),
            shape((slots, feats), dtype),
            [SM] + [VM] * (1 + NY + len(more)),
            flops=flops // 2,
        )(here, near_act, *weights, *more)

    wide = part(0, F32, send(part(1, BF), 0, 1))
    returned = call(leave, payload, [VM] * 2, scratch=scratch)(back, wide)
    home = exchange(returned)

    pieces = call(weights_back, pieces_shape, [SM] + [VM] * 3, flops=flops)(
        here, grad, far_grad, near_act
    )
    joined = [pieces[0]] + [send(pieces[step], step, 0) for step in range(1, NY)]
    weight_grad = call(
        join_gradient, shape((hidden, 2 * NY * feats)), [SM] + [VM] * NY, moved=3 << 20
    )(here, *joined)

    home, weight_grad = lax.optimization_barrier((home, weight_grad))
    combined, back_rows, gate_part = call(
        collect,
        [shape((toks, feats)), shape((rows, hidden)), shape((top, toks), F32)],
        [VM] * 3,
        scratch=scratch,
    )(home, slot, gates_t)
    gate_grad = (gate_part + send(gate_part, 0, 1)).T
    return combined, back_rows.reshape(toks, top, hidden), weight_grad[None], gate_grad


def solution(mesh):
    return jax.shard_map(
        on_device,
        mesh=mesh,
        in_specs=(
            P("expert", None, "dp"),
            P("expert", "dp", None),
            P("expert", None),
            P("expert", "dp"),
            P("expert", None),
            P("expert", None),
            P(),
            P(),
        ),
        out_specs=(
            P("expert", "dp"),
            P("expert", None, "dp"),
            P("expert", "dp", None),
            P("expert", None),
        ),
        check_vma=False,
    )
```

```python
import functools

import jax
import jax.numpy as jnp
from jax import lax
from jax.experimental import pallas as pl
from jax.experimental.pallas import tpu as pltpu
from jax.sharding import PartitionSpec as P

CAP = 3
SLOTS = 2 * CAP
LANES = 128
TILE = 4
NY = 4
EXTRA = 16
BF = jnp.bfloat16
F32 = jnp.float32
VM = pl.BlockSpec(memory_space=pltpu.VMEM)
SM = pl.BlockSpec(memory_space=pltpu.SMEM)


def call(kernel, outs, specs, flops=0, moved=1 << 20, scratch=(), vmem=16 << 20):
    return pl.pallas_call(
        kernel,
        out_shape=outs,
        in_specs=specs,
        out_specs=jax.tree.map(lambda _: VM, outs),
        scratch_shapes=list(scratch),
        compiler_params=pltpu.CompilerParams(vmem_limit_bytes=vmem),
        cost_estimate=pl.CostEstimate(flops=flops, bytes_accessed=moved, transcendentals=0),
    )


def dot(a, b, ca, cb):
    return lax.dot_general(a, b, (((ca,), (cb,)), ((), ())), preferred_element_type=F32)


def shape(dims, dtype=BF):
    return jax.ShapeDtypeStruct(dims, dtype)


def ones(mask):
    return mask.astype(F32).astype(BF)


def iota(dims, axis):
    return lax.broadcasted_iota(jnp.int32, dims, axis)


def payload_rows(feats, hidden):
    wide = SLOTS * feats // LANES
    narrow = -(-SLOTS * hidden // LANES)
    return wide, narrow, -(-(wide + narrow + 1) // TILE) * TILE


def send(value, step, other):
    pairs = [(i, ((i // 2 + step) % NY) * 2 + ((i % 2) ^ other)) for i in range(2 * NY)]
    return lax.ppermute(value, "dp", pairs)


def exchange_y(value):
    groups = [[2 * y + core for y in range(NY)] for core in range(2)]
    return lax.all_to_all(value, "dp", 0, 0, axis_index_groups=groups, tiled=True)


def chip(here, step):
    return lax.rem(here // 2 + step, NY)


def chip_columns(here, step, width):
    return pl.ds(pl.multiple_of(chip(here, step) * width, width), width)


def core_columns(here, other, width):
    core = lax.rem(lax.rem(here, 2) + other, 2)
    return pl.ds(pl.multiple_of(core * width, width), width)


def cut_weights(here_ref, w_ref, *outs):
    width = outs[0].shape[1]
    for step in range(NY):
        outs[step][...] = w_ref[:, chip_columns(here_ref[0], step, width)]


def join_gradient(here_ref, *refs):
    parts, out_ref = refs[:-1], refs[-1]
    width = parts[0].shape[1]
    for step in range(NY):
        columns = chip_columns(here_ref[0], (NY - step) % NY, width)
        out_ref[:, columns] = parts[step][...]


def column(stored):
    top, toks = stored.shape
    spread = jnp.broadcast_to(stored[None], (toks, top, toks)).reshape(toks * top, toks)
    mine = iota(spread.shape, 0) // top == iota(spread.shape, 1)
    return jnp.sum(jnp.where(mine, spread, jnp.zeros_like(spread)), axis=1, keepdims=True)


def as_row(col):
    n = col.shape[0]
    diagonal = iota((n, n), 0) == iota((n, n), 1)
    return jnp.sum(jnp.where(diagonal, col, jnp.zeros_like(col)), axis=0, keepdims=True)


def pack(rows_ref, flat_ref, wide_vals, narrow_vals, scalars=None):
    n_dev = flat_ref.shape[0]
    feats, hidden = wide_vals.shape[1], narrow_vals.shape[1]
    wide, narrow, rows = payload_rows(feats, hidden)
    each = feats // LANES
    for j in range(SLOTS):
        part = slice(j * n_dev, (j + 1) * n_dev)
        for i in range(each):
            block = wide_vals[part, i * LANES : (i + 1) * LANES]
            rows_ref[pl.ds(j * each + i, n_dev, stride=rows), :] = block
        flat_ref[:, j * hidden : (j + 1) * hidden] = narrow_vals[part]
    for i in range(rows - wide):
        block = jnp.zeros((n_dev, LANES), F32)
        if i < narrow:
            block = flat_ref[:, i * LANES : (i + 1) * LANES]
        rows_ref[pl.ds(wide + i, n_dev, stride=rows), :] = block
    if scalars is not None:
        for j in range(SLOTS):
            part = scalars[j * n_dev : (j + 1) * n_dev]
            flat_ref[:, j * EXTRA : (j + 1) * EXTRA] = part
        flat_ref[:, SLOTS * EXTRA : LANES] = jnp.zeros((n_dev, LANES - SLOTS * EXTRA), F32)
        rows_ref[pl.ds(wide + narrow, n_dev, stride=rows), :] = flat_ref[:, :LANES]


def unpack_scalars(rows_ref, n_dev, feats, hidden):
    wide, narrow, rows = payload_rows(feats, hidden)
    block = rows_ref[pl.ds(wide + narrow, n_dev, stride=rows), :]
    return jnp.concatenate([block[:, j * EXTRA : (j + 1) * EXTRA] for j in range(SLOTS)], axis=0)


def two_parts(row):
    high = row.astype(BF).astype(F32)
    at = iota((EXTRA, row.shape[1]), 0)
    return jnp.where(at == 0, high, jnp.where(at == 1, row - high, 0.0))


def unpack(rows_ref, flat_ref, feats, hidden):
    n_dev = flat_ref.shape[0]
    wide, narrow, rows = payload_rows(feats, hidden)
    each = feats // LANES
    wide_vals = jnp.concatenate(
        [
            jnp.concatenate(
                [rows_ref[pl.ds(j * each + i, n_dev, stride=rows), :] for i in range(each)], axis=1
            )
            for j in range(SLOTS)
        ],
        axis=0,
    )
    for i in range(narrow):
        block = rows_ref[pl.ds(wide + i, n_dev, stride=rows), :]
        flat_ref[:, i * LANES : (i + 1) * LANES] = block
    narrow_vals = jnp.concatenate(
        [flat_ref[:, j * hidden : (j + 1) * hidden] for j in range(SLOTS)], axis=0
    )
    return wide_vals, narrow_vals


def dispatch(
    ids_hbm, picks_hbm, place_hbm, cap_hbm, act_hbm, cot_hbm, gate_hbm, sent_ref, slot_ref,
    ids_ref, picks_ref, place_ref, cap_ref, act_ref, cot_ref, gate_ref, rows_ref, flat_ref, sems,
):
    sources = (ids_hbm, picks_hbm, place_hbm, cap_hbm, act_hbm, cot_hbm, gate_hbm)
    targets = (ids_ref, picks_ref, place_ref, cap_ref, act_ref, cot_ref, gate_ref)
    copies = [
        pltpu.make_async_copy(source, target, sems.at[i])
        for i, (source, target) in enumerate(zip(sources, targets))
    ]
    for copy in copies:
        copy.start()
    for copy in copies[:4]:
        copy.wait()
    n_dev = cap_ref.shape[1]
    rows, hidden = act_ref.shape
    toks, feats = cot_ref.shape
    top = rows // toks
    ids, picks = column(ids_ref[...]), column(picks_ref[...])
    match = (place_ref[0:1, :] == ids).astype(jnp.int32)
    has = jnp.sum(match, axis=1, keepdims=True)
    host = jnp.sum(match * place_ref[1:2, :], axis=1, keepdims=True)
    copied = (has > 0) & (picks == 1)
    dest = jnp.where(copied, host, ids)
    dest_row = as_row(dest)
    earlier = (dest == dest_row) & (iota((rows, rows), 1) < iota((rows, rows), 0))
    rank = jnp.sum(earlier.astype(jnp.int32), axis=1, keepdims=True)
    at_dest = iota((rows, n_dev), 1) == dest
    limit = jnp.sum(jnp.where(at_dest, cap_ref[...], 0), axis=1, keepdims=True)
    slot = jnp.where(rank < limit, (jnp.where(copied, CAP, 0) + rank) * n_dev + ids, -1)
    slot_ref[...] = slot
    pick = ones(iota((SLOTS * n_dev, rows), 0) == as_row(slot))
    owner = ones(iota((rows, toks), 0) // top == iota((rows, toks), 1))
    for copy in copies[4:]:
        copy.wait()
    grad = (column(gate_ref[...]) * dot(owner, cot_ref[...], 1, 0)).astype(BF)
    pack(rows_ref, flat_ref, dot(pick, grad, 1, 0), dot(pick, act_ref[...], 1, 0))
    sent_ref[...] = rows_ref[...].astype(BF)


def arrive(got_ref, grad_ref, act_ref, rows_ref, flat_ref):
    rows_ref[...] = got_ref[...].astype(F32)
    grad, acts = unpack(rows_ref, flat_ref, grad_ref.shape[1], act_ref.shape[0])
    grad_ref[...] = grad.astype(BF)
    act_ref[...] = acts.T.astype(BF)


def backward(here_ref, near_ref, far_ref, *refs):
    w_refs, (out_ref, both_ref) = refs[:-2], refs[-2:]
    here, feats = here_ref[0], near_ref.shape[1]
    near, far = core_columns(here, 0, feats), core_columns(here, 1, feats)
    for step in range(NY):
        w_ref = w_refs[step]
        part = dot(w_ref[:, near], near_ref[...], 1, 1) + dot(w_ref[:, far], far_ref[...], 1, 1)
        out_ref[chip(here, step)] = part.astype(BF)
    core = lax.rem(here, 2)
    both_ref[core] = near_ref[...]
    both_ref[1 - core] = far_ref[...]


def seal(here_ref, part_ref, *refs):
    act_refs, out_ref = refs[:-1], refs[-1]
    hidden, slots = act_refs[0].shape
    gate = jnp.zeros((1, slots), F32)
    for step in range(NY):
        at = chip(here_ref[0], step)
        part = part_ref[at]
        products = act_refs[step][...].astype(F32) * part.astype(F32)
        gate = gate + jnp.sum(products, axis=0, keepdims=True)
        out_ref[at, :hidden] = part
    extra = two_parts(gate).astype(BF)
    for y in range(NY):
        out_ref[y, hidden:] = extra


def forward(other, here_ref, *refs):
    act_refs, w_refs, more, out_ref = refs[:NY], refs[NY : 2 * NY], refs[2 * NY : -1], refs[-1]
    columns = core_columns(here_ref[0], other, out_ref.shape[1])
    total = more[0][...].astype(F32) if more else None
    for act_ref, w_ref in zip(act_refs, w_refs):
        part = dot(act_ref[...], w_ref[:, columns], 0, 0)
        total = part if total is None else total + part
    out_ref[...] = total.astype(out_ref.dtype)


def leave(back_ref, wide_ref, sent_ref, rows_ref, flat_ref):
    back = sum(back_ref[y].astype(F32) for y in range(NY))
    hidden = back.shape[0] - EXTRA
    gate = jnp.sum(back[hidden:], axis=0, keepdims=True)
    pack(rows_ref, flat_ref, wide_ref[...], back[:hidden].T, two_parts(gate).T)
    sent_ref[...] = rows_ref[...].astype(BF)


def weights_back(both_ref, *refs):
    feats = both_ref.shape[2]
    for act_ref, out_ref in zip(refs[:NY], refs[NY:]):
        for core in range(2):
            part = dot(act_ref[...], both_ref[core], 1, 0)
            out_ref[:, core * feats : (core + 1) * feats] = part.astype(BF)


def collect(got_ref, slot_ref, gate_ref, mixed_ref, back_ref, gate_out_ref, rows_ref, flat_ref):
    top, toks = gate_ref.shape
    rows, hidden = back_ref.shape
    feats = mixed_ref.shape[1]
    rows_ref[...] = got_ref[...].astype(F32)
    outs, backs = unpack(rows_ref, flat_ref, feats, hidden)
    gate = column(gate_ref[...])
    pick = ones(iota((rows, outs.shape[0]), 1) == slot_ref[...])
    row_out = dot(pick, outs.astype(BF), 1, 0) * gate
    mixed_ref[...] = jnp.sum(row_out.reshape(toks, top, feats), axis=1).astype(BF)
    back = dot(pick, backs.astype(BF), 1, 0)
    back_ref[...] = back.astype(BF)
    scalars = unpack_scalars(rows_ref, flat_ref.shape[0], feats, hidden)
    gate_back = jnp.sum(dot(pick, scalars.astype(BF), 1, 0), axis=1, keepdims=True) / gate
    at_tok = iota((rows, toks), 0) // top == iota((rows, toks), 1)
    spread = jnp.where(at_tok, gate_back, 0.0)
    gate_out_ref[...] = jnp.sum(spread.reshape(toks, top, toks), axis=0)


def on_device(acts, w_down, gates, cotangent, expert_ids, replica_pick, placement, group_cap):
    n_dev = lax.axis_size("expert")
    toks, top, hidden = acts.shape
    feats = cotangent.shape[1]
    rows, slots = toks * top, SLOTS * n_dev
    _, narrow, per_peer = payload_rows(feats, hidden)
    payload = shape((n_dev * per_peer, LANES))
    scratch = [
        pltpu.VMEM((n_dev * per_peer, LANES), F32),
        pltpu.VMEM((n_dev, narrow * LANES), F32),
    ]
    here = lax.axis_index("dp").astype(jnp.int32).reshape(1)
    gates_t = gates.T
    pieces_shape = [shape((hidden, 2 * feats))] * NY

    cuts = call(cut_weights, pieces_shape, [SM, VM], moved=3 << 20)(here, w_down[0])
    weights = [cuts[0]] + [send(cuts[NY - step], NY - step, 0) for step in range(1, NY)]

    inputs = (
        expert_ids.T, replica_pick.T, placement.T, group_cap.reshape(1, n_dev),
        acts.reshape(rows, hidden), cotangent, gates_t,
    )
    sent, slot = call(
        dispatch,
        [payload, shape((rows, 1), jnp.int32)],
        [pl.BlockSpec(memory_space=pltpu.HBM)] * len(inputs),
        scratch=[pltpu.VMEM(x.shape, x.dtype) for x in inputs]
        + scratch
        + [pltpu.SemaphoreType.DMA((len(inputs),))],
        vmem=63 << 20,
    )(*inputs)

    def exchange(value):
        value = value.reshape(n_dev, per_peer // TILE, TILE, LANES)
        return lax.all_to_all(value, "expert", 0, 0, tiled=True).reshape(payload.shape)

    got = exchange(sent)
    flops = 2 * slots * feats * hidden * 2 * NY
    grad, own_act = call(
        arrive, [shape((slots, feats)), shape((hidden, slots))], [VM], scratch=scratch
    )(got)
    far_grad = send(grad, 0, 1)
    all_acts = [own_act] + [send(own_act, NY - step, 0) for step in range(1, NY)]
    parts, both = call(
        backward,
        [shape((NY, hidden, slots)), shape((2, slots, feats))],
        [SM] + [VM] * (2 + NY),
        flops=flops,
    )(here, grad, far_grad, *weights)
    back = call(seal, shape((NY, hidden + EXTRA, slots)), [SM] + [VM] * (1 + NY))(
        here, parts, *all_acts
    )
    back = exchange_y(back)

    def part(other, dtype, *more):
        return call(
            functools.partial(forward, other),
            shape((slots, feats), dtype),
            [SM] + [VM] * (2 * NY + len(more)),
            flops=flops // 2,
        )(here, *all_acts, *weights, *more)

    wide = part(0, F32, send(part(1, BF), 0, 1))
    returned = call(leave, payload, [VM] * 2, scratch=scratch)(back, wide)
    home = exchange(returned)

    pieces = call(weights_back, pieces_shape, [VM] * (1 + NY), flops=flops)(both, *all_acts)
    joined = [pieces[0]] + [send(pieces[step], step, 0) for step in range(1, NY)]
    weight_grad = call(
        join_gradient, shape((hidden, 2 * NY * feats)), [SM] + [VM] * NY, moved=3 << 20
    )(here, *joined)

    home, weight_grad = lax.optimization_barrier((home, weight_grad))
    combined, back_rows, gate_part = call(
        collect,
        [shape((toks, feats)), shape((rows, hidden)), shape((top, toks), F32)],
        [VM] * 3,
        scratch=scratch,
    )(home, slot, gates_t)
    gate_grad = (gate_part + send(gate_part, 0, 1)).T
    return combined, back_rows.reshape(toks, top, hidden), weight_grad[None], gate_grad


def solution(mesh):
    return jax.shard_map(
        on_device,
        mesh=mesh,
        in_specs=(
            P("expert", None, "dp"),
            P("expert", "dp", None),
            P("expert", None),
            P("expert", "dp"),
            P("expert", None),
            P("expert", None),
            P(),
            P(),
        ),
        out_specs=(
            P("expert", "dp"),
            P("expert", None, "dp"),
            P("expert", "dp", None),
            P("expert", None),
        ),
        check_vma=False,
    )
```

```python
import functools

import jax
import jax.numpy as jnp
from jax import lax
from jax.experimental import pallas as pl
from jax.experimental.pallas import tpu as pltpu
from jax.sharding import PartitionSpec as P

CAP = 3
SLOTS = 2 * CAP
LANES = 128
TILE = 4
NY = 4
BF = jnp.bfloat16
F32 = jnp.float32
VM = pl.BlockSpec(memory_space=pltpu.VMEM)
SM = pl.BlockSpec(memory_space=pltpu.SMEM)


def call(kernel, outs, specs, flops=0, moved=1 << 20, scratch=(), vmem=16 << 20):
    return pl.pallas_call(
        kernel,
        out_shape=outs,
        in_specs=specs,
        out_specs=jax.tree.map(lambda _: VM, outs),
        scratch_shapes=list(scratch),
        compiler_params=pltpu.CompilerParams(vmem_limit_bytes=vmem),
        cost_estimate=pl.CostEstimate(flops=flops, bytes_accessed=moved, transcendentals=0),
    )


def dot(a, b, ca, cb):
    return lax.dot_general(a, b, (((ca,), (cb,)), ((), ())), preferred_element_type=F32)


def shape(dims, dtype=BF):
    return jax.ShapeDtypeStruct(dims, dtype)


def ones(mask):
    return mask.astype(F32).astype(BF)


def iota(dims, axis):
    return lax.broadcasted_iota(jnp.int32, dims, axis)


def payload_rows(feats, hidden):
    wide = SLOTS * feats // LANES
    narrow = -(-SLOTS * hidden // LANES)
    return wide, narrow, -(-(wide + narrow) // TILE) * TILE


def send(value, step, other):
    pairs = [(i, ((i // 2 + step) % NY) * 2 + ((i % 2) ^ other)) for i in range(2 * NY)]
    return lax.ppermute(value, "dp", pairs)


def exchange_y(value):
    groups = [[2 * y + core for y in range(NY)] for core in range(2)]
    return lax.all_to_all(value, "dp", 0, 0, axis_index_groups=groups, tiled=True)


def chip(here, step):
    return lax.rem(here // 2 + step, NY)


def chip_columns(here, step, width):
    return pl.ds(pl.multiple_of(chip(here, step) * width, width), width)


def core_columns(here, other, width):
    core = lax.rem(lax.rem(here, 2) + other, 2)
    return pl.ds(pl.multiple_of(core * width, width), width)


def cut_weights(here_ref, w_ref, *outs):
    width = outs[0].shape[1]
    for step in range(NY):
        outs[step][...] = w_ref[:, chip_columns(here_ref[0], step, width)]


def join_gradient(here_ref, *refs):
    parts, out_ref = refs[:-1], refs[-1]
    width = parts[0].shape[1]
    for step in range(NY):
        columns = chip_columns(here_ref[0], (NY - step) % NY, width)
        out_ref[:, columns] = parts[step][...]


def column(stored):
    top, toks = stored.shape
    spread = jnp.broadcast_to(stored[None], (toks, top, toks)).reshape(toks * top, toks)
    mine = iota(spread.shape, 0) // top == iota(spread.shape, 1)
    return jnp.sum(jnp.where(mine, spread, jnp.zeros_like(spread)), axis=1, keepdims=True)


def as_row(col):
    n = col.shape[0]
    diagonal = iota((n, n), 0) == iota((n, n), 1)
    return jnp.sum(jnp.where(diagonal, col, jnp.zeros_like(col)), axis=0, keepdims=True)


def pack(rows_ref, flat_ref, wide_vals, narrow_vals):
    n_dev = flat_ref.shape[0]
    feats, hidden = wide_vals.shape[1], narrow_vals.shape[1]
    wide, narrow, rows = payload_rows(feats, hidden)
    each = feats // LANES
    for j in range(SLOTS):
        part = slice(j * n_dev, (j + 1) * n_dev)
        for i in range(each):
            block = wide_vals[part, i * LANES : (i + 1) * LANES]
            rows_ref[pl.ds(j * each + i, n_dev, stride=rows), :] = block
        flat_ref[:, j * hidden : (j + 1) * hidden] = narrow_vals[part]
    for i in range(rows - wide):
        block = jnp.zeros((n_dev, LANES), F32)
        if i < narrow:
            block = flat_ref[:, i * LANES : (i + 1) * LANES]
        rows_ref[pl.ds(wide + i, n_dev, stride=rows), :] = block


def unpack(rows_ref, flat_ref, feats, hidden):
    n_dev = flat_ref.shape[0]
    wide, narrow, rows = payload_rows(feats, hidden)
    each = feats // LANES
    wide_vals = jnp.concatenate(
        [
            jnp.concatenate(
                [rows_ref[pl.ds(j * each + i, n_dev, stride=rows), :] for i in range(each)], axis=1
            )
            for j in range(SLOTS)
        ],
        axis=0,
    )
    for i in range(narrow):
        block = rows_ref[pl.ds(wide + i, n_dev, stride=rows), :]
        flat_ref[:, i * LANES : (i + 1) * LANES] = block
    narrow_vals = jnp.concatenate(
        [flat_ref[:, j * hidden : (j + 1) * hidden] for j in range(SLOTS)], axis=0
    )
    return wide_vals, narrow_vals


def dispatch(
    ids_hbm, picks_hbm, place_hbm, cap_hbm, act_hbm, cot_hbm, gate_hbm, sent_ref, slot_ref,
    ids_ref, picks_ref, place_ref, cap_ref, act_ref, cot_ref, gate_ref, rows_ref, flat_ref, sems,
):
    sources = (ids_hbm, picks_hbm, place_hbm, cap_hbm, act_hbm, cot_hbm, gate_hbm)
    targets = (ids_ref, picks_ref, place_ref, cap_ref, act_ref, cot_ref, gate_ref)
    copies = [
        pltpu.make_async_copy(source, target, sems.at[i])
        for i, (source, target) in enumerate(zip(sources, targets))
    ]
    for copy in copies:
        copy.start()
    for copy in copies[:4]:
        copy.wait()
    n_dev = cap_ref.shape[1]
    rows, hidden = act_ref.shape
    toks, feats = cot_ref.shape
    top = rows // toks
    ids, picks = column(ids_ref[...]), column(picks_ref[...])
    match = (place_ref[0:1, :] == ids).astype(jnp.int32)
    has = jnp.sum(match, axis=1, keepdims=True)
    host = jnp.sum(match * place_ref[1:2, :], axis=1, keepdims=True)
    copied = (has > 0) & (picks == 1)
    dest = jnp.where(copied, host, ids)
    dest_row = as_row(dest)
    earlier = (dest == dest_row) & (iota((rows, rows), 1) < iota((rows, rows), 0))
    rank = jnp.sum(earlier.astype(jnp.int32), axis=1, keepdims=True)
    at_dest = iota((rows, n_dev), 1) == dest
    limit = jnp.sum(jnp.where(at_dest, cap_ref[...], 0), axis=1, keepdims=True)
    slot = jnp.where(rank < limit, (jnp.where(copied, CAP, 0) + rank) * n_dev + ids, -1)
    slot_ref[...] = slot
    pick = ones(iota((SLOTS * n_dev, rows), 0) == as_row(slot))
    owner = ones(iota((rows, toks), 0) // top == iota((rows, toks), 1))
    for copy in copies[4:]:
        copy.wait()
    grad = (column(gate_ref[...]) * dot(owner, cot_ref[...], 1, 0)).astype(BF)
    pack(rows_ref, flat_ref, dot(pick, grad, 1, 0), dot(pick, act_ref[...], 1, 0))
    sent_ref[...] = rows_ref[...].astype(BF)


def arrive(got_ref, grad_ref, act_ref, rows_ref, flat_ref):
    rows_ref[...] = got_ref[...].astype(F32)
    grad, acts = unpack(rows_ref, flat_ref, grad_ref.shape[1], act_ref.shape[0])
    grad_ref[...] = grad.astype(BF)
    act_ref[...] = acts.T.astype(BF)


def backward(here_ref, near_ref, far_ref, *refs):
    w_refs, (out_ref, both_ref) = refs[:-2], refs[-2:]
    here, feats = here_ref[0], near_ref.shape[1]
    near, far = core_columns(here, 0, feats), core_columns(here, 1, feats)
    for step in range(NY):
        w_ref = w_refs[step]
        part = dot(w_ref[:, near], near_ref[...], 1, 1) + dot(w_ref[:, far], far_ref[...], 1, 1)
        out_ref[chip(here, step)] = part.astype(BF)
    core = lax.rem(here, 2)
    both_ref[core] = near_ref[...]
    both_ref[1 - core] = far_ref[...]


def forward(other, here_ref, *refs):
    act_refs, w_refs, more, out_ref = refs[:NY], refs[NY : 2 * NY], refs[2 * NY : -1], refs[-1]
    columns = core_columns(here_ref[0], other, out_ref.shape[1])
    total = more[0][...].astype(F32) if more else None
    for act_ref, w_ref in zip(act_refs, w_refs):
        part = dot(act_ref[...], w_ref[:, columns], 0, 0)
        total = part if total is None else total + part
    out_ref[...] = total.astype(out_ref.dtype)


def leave(back_ref, wide_ref, sent_ref, rows_ref, flat_ref):
    back = sum(back_ref[y].astype(F32) for y in range(NY))
    pack(rows_ref, flat_ref, wide_ref[...], back.T)
    sent_ref[...] = rows_ref[...].astype(BF)


def weights_back(both_ref, *refs):
    feats = both_ref.shape[2]
    for act_ref, out_ref in zip(refs[:NY], refs[NY:]):
        for core in range(2):
            part = dot(act_ref[...], both_ref[core], 1, 0)
            out_ref[:, core * feats : (core + 1) * feats] = part.astype(BF)


def collect(got_ref, slot_ref, gate_ref, act_ref, mixed_ref, back_ref, gate_out_ref, rows_ref, flat_ref):
    top, toks = gate_ref.shape
    rows, hidden = back_ref.shape
    feats = mixed_ref.shape[1]
    rows_ref[...] = got_ref[...].astype(F32)
    outs, backs = unpack(rows_ref, flat_ref, feats, hidden)
    gate = column(gate_ref[...])
    pick = ones(iota((rows, outs.shape[0]), 1) == slot_ref[...])
    row_out = dot(pick, outs.astype(BF), 1, 0) * gate
    mixed_ref[...] = jnp.sum(row_out.reshape(toks, top, feats), axis=1).astype(BF)
    back = dot(pick, backs.astype(BF), 1, 0)
    back_ref[...] = back.astype(BF)
    gate_back = jnp.sum(back * act_ref[...].astype(F32), axis=1, keepdims=True) / gate
    at_tok = iota((rows, toks), 0) // top == iota((rows, toks), 1)
    spread = jnp.where(at_tok, gate_back, 0.0)
    gate_out_ref[...] = jnp.zeros_like(gate_out_ref)
    part = jnp.sum(spread.reshape(toks, top, toks), axis=0)
    for i in range(2 * NY):
        gate_out_ref[i, :, :toks] = part


def on_device(acts, w_down, gates, cotangent, expert_ids, replica_pick, placement, group_cap):
    n_dev = lax.axis_size("expert")
    toks, top, hidden = acts.shape
    feats = cotangent.shape[1]
    rows, slots = toks * top, SLOTS * n_dev
    _, narrow, per_peer = payload_rows(feats, hidden)
    payload = shape((n_dev * per_peer, LANES))
    scratch = [
        pltpu.VMEM((n_dev * per_peer, LANES), F32),
        pltpu.VMEM((n_dev, narrow * LANES), F32),
    ]
    here = lax.axis_index("dp").astype(jnp.int32).reshape(1)
    gates_t = gates.T
    pieces_shape = [shape((hidden, 2 * feats))] * NY

    cuts = call(cut_weights, pieces_shape, [SM, VM], moved=3 << 20)(here, w_down[0])
    weights = [cuts[0]] + [send(cuts[NY - step], NY - step, 0) for step in range(1, NY)]

    inputs = (
        expert_ids.T, replica_pick.T, placement.T, group_cap.reshape(1, n_dev),
        acts.reshape(rows, hidden), cotangent, gates_t,
    )
    sent, slot = call(
        dispatch,
        [payload, shape((rows, 1), jnp.int32)],
        [pl.BlockSpec(memory_space=pltpu.HBM)] * len(inputs),
        scratch=[pltpu.VMEM(x.shape, x.dtype) for x in inputs]
        + scratch
        + [pltpu.SemaphoreType.DMA((len(inputs),))],
        vmem=63 << 20,
    )(*inputs)

    def exchange(value):
        value = value.reshape(n_dev, per_peer // TILE, TILE, LANES)
        return lax.all_to_all(value, "expert", 0, 0, tiled=True).reshape(payload.shape)

    got = exchange(sent)
    flops = 2 * slots * feats * hidden * 2 * NY
    grad, own_act = call(
        arrive, [shape((slots, feats)), shape((hidden, slots))], [VM], scratch=scratch
    )(got)
    far_grad = send(grad, 0, 1)
    all_acts = [own_act] + [send(own_act, NY - step, 0) for step in range(1, NY)]
    parts, both = call(
        backward,
        [shape((NY, hidden, slots)), shape((2, slots, feats))],
        [SM] + [VM] * (2 + NY),
        flops=flops,
    )(here, grad, far_grad, *weights)
    back = exchange_y(parts)

    def part(other, dtype, *more):
        return call(
            functools.partial(forward, other),
            shape((slots, feats), dtype),
            [SM] + [VM] * (2 * NY + len(more)),
            flops=flops // 2,
        )(here, *all_acts, *weights, *more)

    wide = part(0, F32, send(part(1, BF), 0, 1))
    returned = call(leave, payload, [VM] * 2, scratch=scratch)(back, wide)
    home = exchange(returned)

    pieces = call(weights_back, pieces_shape, [VM] * (1 + NY), flops=flops)(both, *all_acts)
    joined = [pieces[0]] + [send(pieces[step], step, 0) for step in range(1, NY)]
    weight_grad = call(
        join_gradient, shape((hidden, 2 * NY * feats)), [SM] + [VM] * NY, moved=3 << 20
    )(here, *joined)

    home, weight_grad = lax.optimization_barrier((home, weight_grad))
    combined, back_rows, gate_parts = call(
        collect,
        [shape((toks, feats)), shape((rows, hidden)), shape((2 * NY, top, LANES), F32)],
        [VM] * 4,
        scratch=scratch,
    )(home, slot, gates_t, inputs[4])
    gate_parts = lax.all_to_all(gate_parts, "dp", 0, 0, tiled=True)
    gate_grad = jnp.sum(gate_parts, axis=0)[:, :toks].T
    return combined, back_rows.reshape(toks, top, hidden), weight_grad[None], gate_grad


def solution(mesh):
    return jax.shard_map(
        on_device,
        mesh=mesh,
        in_specs=(
            P("expert", None, "dp"),
            P("expert", "dp", None),
            P("expert", None),
            P("expert", "dp"),
            P("expert", None),
            P("expert", None),
            P(),
            P(),
        ),
        out_specs=(
            P("expert", "dp"),
            P("expert", None, "dp"),
            P("expert", "dp", None),
            P("expert", None),
        ),
        check_vma=False,
    )
```
